32 devices in a mesh: tower: 2 (over core), group: 4 (over y, x), blk: 4 (over z).
Axes of the slice: x: 2, y: 2, z: 4, core: 2. Of those that a mesh axis runs over, the one named last changes fastest.
Arguments:
- queries: bfloat16 [128, 384, 256], P(('tower', 'group', 'blk')), may hold values from -102 to 102
- cluster_ids: int32 [128, 64], P(('tower', 'group', 'blk')), may hold values from 0 to 127, all different within a row
- positives: int32 [128, 384], P(('tower', 'group', 'blk')), may hold values from 0 to 1023
- owner_map: int32 [4, 128], P('group'), may hold values from 0 to 127, each once within a row
- panels: bfloat16 [512, 16, 256], P(('group', 'blk')), may hold values from -0.375 to 0.375
- scales: bfloat16 [512, 16], P(('group', 'blk')), may hold values from 0.5 to 2
Outputs:
- losses: bfloat16 [128, 384], P(('tower', 'group', 'blk'))
- query_grads: bfloat16 [128, 384, 256], P(('tower', 'group', 'blk'))
- panel_grads: float32 [512, 16, 256], P(('group', 'blk'), 'tower')
The draws below stay inside these ranges and needn't reach their ends.
Inputs may be any that keep to these rules, and one draw needn't show every extreme that they name: `cluster_ids`: each row lists 64 different clusters. `owner_map`: each row is a permutation.
All inputs are finite; a program needn't handle non-finite values.
Results may differ from the reference program's by a relative error of at most 0.014.
Values may be sent and summed in bfloat16 or wider, within the bound.
No kernel may reach another device: no remote copies, remote signals or barrier semaphores. Data moves between devices by JAX's collectives and lax.ppermute only.
A program may use at most 64 MiB of HBM per device.

```python
import math
import jax
import jax.numpy as jnp
from jax import lax

D = 256
ITEMS = 16
NSEL = 64
CLG = 128
QB = 384
BPG = 1
NQB = 128
NCL = 512
N_GROUP = 4


def draw_queries(key, part):
    subkeys = jax.random.split(key, 1)
    shape = (NQB, QB, D)
    values = jnp.clip(jax.random.normal(subkeys[0], shape, jnp.float32), -6.0, 6.0)
    return values.astype(jnp.bfloat16)


def set_ends(values, stream_key, low, largest):
    longest = values.shape.index(max(values.shape))
    spots = []
    for shift in (0, 1):
        where = [jax.random.randint(jax.random.fold_in(stream_key, axis), (), 0, length) for axis, length in enumerate(values.shape)]
        where[longest] = (where[longest] + shift) % values.shape[longest]
        spots.append(tuple(where))
    return values.at[spots[0]].set(low).at[spots[1]].set(largest)


def steps_of(key, dims, pieces, least, largest):
    factor_of = 1.0
    for dim, shards_of in pieces:
        heights = jax.random.uniform(jax.random.fold_in(jax.random.fold_in(key, 6), dim), (shards_of,), jnp.float32, least / len(pieces), largest / len(pieces))
        factor_of = factor_of * jnp.repeat(jnp.exp(heights), dims[dim] // shards_of).reshape((-1,) + (1,) * (len(dims) - 1 - dim))
    return factor_of


def choose_distinct(rng, rows, count, top, lift):
    ranking = jax.random.permutation(jax.random.fold_in(rng, 1), count)
    boost = ranking
    for power in range(3):
        boost = boost * boost // count
    boost = boost * lift // count
    lots = jax.random.randint(jax.random.fold_in(rng, 2), (rows, count), 0, 4096) + boost
    sure = jax.random.permutation(jax.random.fold_in(rng, 3), rows)[jnp.arange(count) % rows]
    lots = jnp.where(jnp.arange(rows)[:, None] == sure[None, :], 1 << 14, lots)
    score = lots * count + jnp.arange(count)
    return lax.top_k(score.astype(jnp.int32), top)[1].astype(jnp.int32)


def normal_values(rng, extent, width, most, cuts=(), held_as=jnp.bfloat16):
    array = jax.random.normal(rng, extent, jnp.float32) * width
    if len(cuts) > 0:
        array = steps_of(rng, extent, cuts, -0.22, 0.18) * array
    return jnp.clip(array, min=-most, max=most).astype(held_as)


def setup_inputs(seed: int = 0) -> dict:
    keys = jax.random.split(jax.random.key(seed), 7)
    return {
        "queries": draw_queries(jax.random.fold_in(keys[6], 71), 0),
        "cluster_ids": choose_distinct(keys[1], NQB, CLG, NSEL, 8192),
        "positives": set_ends(jax.random.randint(keys[2], (NQB, QB), 0, NSEL * ITEMS), jax.random.fold_in(keys[2], 1), 0, (NSEL * ITEMS) - 1).astype(jnp.int32),
        "owner_map": jax.vmap(lambda own: jax.random.permutation(own, CLG))(jax.random.split(keys[3], N_GROUP)).reshape((N_GROUP, CLG)).astype(jnp.int32),
        "panels": normal_values(keys[4], (NCL, ITEMS, D), D ** -0.5, 0.375, ((0, 16),)),
        "scales": jnp.clip(jnp.exp(math.log(2.0) - 1.3862944 * jax.random.uniform(keys[5], (NCL, ITEMS), jnp.float32) ** steps_of(keys[5], (NCL, ITEMS), ((0, 16),), -0.2, 0.2)), 0.5, 2.0).astype(jnp.bfloat16),
    }


def reference(queries, cluster_ids, positives, owner_map, panels, scales):
    block_dev = BPG * N_GROUP

    def one_block(panel_grads, inputs):
        block_query, block_ids, block_pos, block_index = inputs
        group_index = (block_index % block_dev) // BPG
        panel_slots = owner_map[group_index][block_ids]
        clusters = (group_index * CLG + panel_slots).astype(jnp.int32)
        candidates = panels[clusters].reshape(NSEL * ITEMS, D)
        cand_scale = scales[clusters].reshape(NSEL * ITEMS).astype(jnp.float32)
        scores = jnp.dot(block_query, candidates.T, preferred_element_type=jnp.float32) * cand_scale[None, :]
        row_peak = jnp.max(scores, axis=1, keepdims=True)
        log_total = row_peak[:, 0] + jnp.log(jnp.sum(jnp.exp(scores - row_peak), axis=1))
        picked = jnp.take_along_axis(scores, block_pos[:, None], axis=1)[:, 0]
        losses = (log_total - picked).astype(jnp.bfloat16)
        onehot = (jnp.arange(NSEL * ITEMS, dtype=jnp.int32)[None, :] == block_pos[:, None]).astype(jnp.float32)
        weights = ((jnp.exp(scores - log_total[:, None]) - onehot) * cand_scale[None, :]).astype(jnp.bfloat16)
        query_grad = jnp.dot(weights, candidates, preferred_element_type=jnp.float32).astype(jnp.bfloat16)
        grad_term = jnp.dot(weights.T, block_query, preferred_element_type=jnp.float32).reshape(NSEL, ITEMS, D)
        panel_grads = panel_grads.at[clusters].add(grad_term)
        return panel_grads, (losses, query_grad)

    zero_grads = jnp.zeros((NCL, ITEMS, D), jnp.float32)
    indices = jnp.arange(NQB, dtype=jnp.int32)
    panel_grads, (losses, query_grads) = lax.scan(one_block, zero_grads, (queries, cluster_ids, positives, indices))
    return losses, query_grads, panel_grads
```

```python
import functools

import jax
import jax.numpy as jnp
from jax import lax
from jax.experimental import pallas as pl
from jax.experimental.pallas import tpu as pltpu
from jax.sharding import PartitionSpec as P

VMEM_LIMIT = 48 * 1024 * 1024
LANES = 128
TILE = 16


def peers(axis):
    n = lax.axis_size(axis)
    me = lax.axis_index(axis)
    if n & (n - 1) == 0:
        return [(me ^ k, me ^ k, [(i, i ^ k) for i in range(n)]) for k in range(1, n)]
    return [
        (lax.rem(me + k, n), lax.rem(me + n - k, n), [(i, (i + k) % n) for i in range(n)])
        for k in range(1, n)
    ]


def pick(array, index):
    return lax.dynamic_index_in_dim(array, index, 0, keepdims=False)


def weights_kernel(dims, *refs):
    (nq, nblk, ntow, rows, nsel, items, slots, shard) = dims
    meta, pos_ref = refs[0], refs[1]
    q_refs = refs[2 : 2 + nq]
    own_ref, own_scale = refs[2 + nq], refs[3 + nq]
    n_piece = (nblk - 1) * ntow
    pieces = refs[4 + nq : 4 + nq + n_piece]
    w_ref, sel_ref, loss_ref, grad_ref = refs[4 + nq + n_piece : 8 + nq + n_piece]
    panel, scale, wide, score, sel_wide, term = refs[8 + nq + n_piece :]
    part = shard // ntow
    cand = nsel * items
    row0 = nq * nsel

    own_start = pl.multiple_of(meta[row0] * (shard * items), TILE)
    panel[pl.ds(own_start, shard * items), :] = own_ref[...]
    scale[...] = jnp.zeros_like(scale)
    scale[pl.ds(pl.multiple_of(meta[row0] * shard, 8), shard), 0:items] = own_scale[...].astype(
        jnp.float32
    )
    for n, piece in enumerate(pieces):
        first = meta[row0 + 1 + n]
        panel[pl.ds(pl.multiple_of(first * items, TILE), part * items), :] = piece[
            0 : part * items, :
        ]
        scale[pl.ds(first, part), :] = piece[
            part * items : part * items + part, 0:LANES
        ].astype(jnp.float32)

    total = slots * items
    slot_of = lax.broadcasted_iota(jnp.int32, (total, slots), 0) // items
    spread = (slot_of == lax.broadcasted_iota(jnp.int32, (total, slots), 1)).astype(jnp.bfloat16)
    by_slot = jnp.dot(
        spread, scale[...].astype(jnp.bfloat16), preferred_element_type=jnp.float32
    )
    item_of = lax.broadcasted_iota(jnp.int32, (total, LANES), 0) % items
    own_item = item_of == lax.broadcasted_iota(jnp.int32, (total, LANES), 1)
    wide[...] = jnp.dot(
        jnp.where(own_item, by_slot, 0.0).astype(jnp.bfloat16),
        jnp.ones((LANES, LANES), jnp.bfloat16),
        preferred_element_type=jnp.float32,
    )
    grad_ref[...] = jnp.zeros_like(grad_ref)

    step = 64
    reps = rows // LANES
    for b in range(nq):
        for j in range(nsel):
            start = pl.multiple_of(meta[b * nsel + j] * items, TILE)
            sel_ref[b, j * items : (j + 1) * items, :] = panel[pl.ds(start, items), :]
            sel_wide[j * items : (j + 1) * items, :] = wide[pl.ds(start, items), :]
        query = q_refs[b][...]
        score[...] = lax.dot_general(
            sel_ref[b],
            query,
            (((1,), (1,)), ((), ())),
            preferred_element_type=jnp.float32,
        )
        pos = pos_ref[b : b + 1, :]

        def scaled(c, peak):
            at = pl.ds(pl.multiple_of(c * step, step), step)
            s = score[at, :] * jnp.tile(sel_wide[at, :], (1, reps))
            score[at, :] = s
            return jnp.maximum(peak, jnp.max(s.reshape(step // 8, 8, rows), axis=0))

        peak8 = lax.fori_loop(
            0, cand // step, scaled, jnp.full((8, rows), -jnp.inf, jnp.float32), unroll=True
        )
        peak = jnp.max(peak8, axis=0, keepdims=True)

        def exps(c, carry):
            total8, pick8 = carry
            at = pl.ds(pl.multiple_of(c * step, step), step)
            s = score[at, :]
            hot = lax.broadcasted_iota(jnp.int32, (step, rows), 0) == pos - c * step
            e = jnp.exp(s - peak)
            score[at, :] = e
            picked = jnp.where(hot, s, 0.0)
            return (
                total8 + jnp.sum(e.reshape(step // 8, 8, rows), axis=0),
                pick8 + jnp.sum(picked.reshape(step // 8, 8, rows), axis=0),
            )

        zero8 = jnp.zeros((8, rows), jnp.float32)
        total8, pick8 = lax.fori_loop(0, cand // step, exps, (zero8, zero8), unroll=True)
        total = jnp.sum(total8, axis=0, keepdims=True)
        picked = jnp.sum(pick8, axis=0, keepdims=True)
        loss_ref[b : b + 1, :] = peak + jnp.log(total) - picked
        inverse = 1.0 / total

        def weigh(c, _):
            at = pl.ds(pl.multiple_of(c * step, step), step)
            hot = lax.broadcasted_iota(jnp.int32, (step, rows), 0) == pos - c * step
            chance = score[at, :] * inverse - jnp.where(hot, 1.0, 0.0)
            w = chance * jnp.tile(sel_wide[at, :], (1, reps))
            w_ref[b, at, :] = w.astype(jnp.bfloat16)
            return 0

        lax.fori_loop(0, cand // step, weigh, 0, unroll=True)
        term[...] = jnp.dot(w_ref[b], query, preferred_element_type=jnp.float32)
        for j in range(nsel):
            start = pl.multiple_of(meta[b * nsel + j] * items, TILE)
            grad_ref[pl.ds(start, items), :] += term[j * items : (j + 1) * items, :]


def query_kernel(nq, w_ref, sel_ref, *outs):
    for b in range(nq):
        outs[b][...] = lax.dot_general(
            w_ref[b],
            sel_ref[b],
            (((0,), (0,)), ((), ())),
            preferred_element_type=jnp.float32,
        ).astype(jnp.bfloat16)


def shards(queries, cluster_ids, positives, owner_map, panels, scales):
    nq, rows, width = queries.shape
    shard, items = scales.shape
    nsel = cluster_ids.shape[1]
    nblk, ntow = lax.axis_size("blk"), lax.axis_size("tower")
    slots = shard * nblk
    part = shard // ntow
    cand = nsel * items
    mine, blk_me, tow_me = lax.axis_index("group"), lax.axis_index("blk"), lax.axis_index("tower")
    group_peers, blk_peers, tow_peers = peers("group"), peers("blk"), peers("tower")
    per = nq // lax.axis_size("group")

    flat_scales = jnp.pad(scales, ((0, 0), (0, width - items)))
    half = lax.dynamic_slice_in_dim(panels, tow_me * part, part, 0).reshape(part * items, width)
    half_scales = lax.dynamic_slice_in_dim(flat_scales, tow_me * part, part, 0)
    pad_rows = -part % TILE
    message = jnp.concatenate([half, half_scales, jnp.zeros((pad_rows, width), half.dtype)])
    pieces, firsts = [], []
    for to, source, pattern in blk_peers:
        piece = lax.ppermute(message, "blk", pattern)
        pieces.append(piece)
        firsts.append(source * shard + tow_me * part)
        for _, tow_source, tow_pattern in tow_peers:
            pieces.append(lax.ppermute(piece, "tower", tow_pattern))
            firsts.append(source * shard + tow_source * part)

    blocks = queries.reshape(nq // per, per, rows, width)
    lists = jnp.concatenate([cluster_ids, positives], axis=1).reshape(nq // per, per, nsel + rows)
    got_q, got_l = [pick(blocks, mine)], [pick(lists, mine)]
    for to, source, pattern in group_peers:
        got_l.append(lax.ppermute(pick(lists, to), "group", pattern))
        got_q.append(lax.ppermute(pick(blocks, to), "group", pattern))
    q_list = [q[i] for q in got_q for i in range(per)]
    got = jnp.concatenate(got_l, axis=0)
    ids, pos = got[:, :nsel], got[:, nsel:]
    hot = ids[:, :, None] == lax.iota(jnp.int32, slots)[None, None, :]
    listed = jnp.sum(jnp.where(hot, owner_map[0][None, None, :], 0), axis=2)
    meta = jnp.concatenate(
        [listed.reshape(-1), jnp.stack([blk_me] + firsts).astype(jnp.int32)]
    )

    vmem = pl.BlockSpec(memory_space=pltpu.VMEM)
    smem = pl.BlockSpec(memory_space=pltpu.SMEM)
    dims = (nq, nblk, ntow, rows, nsel, items, slots, shard)
    w, sel, loss, grads = pl.pallas_call(
        functools.partial(weights_kernel, dims),
        out_shape=(
            jax.ShapeDtypeStruct((nq, cand, rows), jnp.bfloat16),
            jax.ShapeDtypeStruct((nq, cand, width), jnp.bfloat16),
            jax.ShapeDtypeStruct((nq, rows), jnp.float32),
            jax.ShapeDtypeStruct((slots * items, width), jnp.float32),
        ),
        in_specs=[smem] + [vmem] * (3 + nq + len(pieces)),
        out_specs=(vmem,) * 4,
        scratch_shapes=[
            pltpu.VMEM((slots * items, width), jnp.bfloat16),
            pltpu.VMEM((slots, LANES), jnp.float32),
            pltpu.VMEM((slots * items, LANES), jnp.float32),
            pltpu.VMEM((cand, rows), jnp.float32),
            pltpu.VMEM((cand, LANES), jnp.float32),
            pltpu.VMEM((cand, width), jnp.float32),
        ],
        compiler_params=pltpu.CompilerParams(vmem_limit_bytes=VMEM_LIMIT),
        name="weights",
    )(meta, pos, *q_list, panels.reshape(shard * items, width), scales, *pieces)

    by_part = grads.reshape(slots, ntow, items // ntow, width)
    total = lax.dynamic_index_in_dim(by_part, tow_me, 1, keepdims=False)
    for to, source, pattern in tow_peers:
        sent = lax.dynamic_index_in_dim(by_part, to, 1, keepdims=False).astype(jnp.bfloat16)
        total = total + lax.ppermute(sent, "tower", pattern).astype(jnp.float32)
    by_shard = total.reshape(nblk, shard, items // ntow, width)

    query_grads = pl.pallas_call(
        functools.partial(query_kernel, nq),
        out_shape=[jax.ShapeDtypeStruct((rows, width), jnp.bfloat16)] * nq,
        in_specs=[vmem, vmem],
        out_specs=[vmem] * nq,
        compiler_params=pltpu.CompilerParams(vmem_limit_bytes=VMEM_LIMIT),
        name="query_grads",
    )(w, sel)

    panel_grads = pick(by_shard, blk_me)
    for to, source, pattern in blk_peers:
        sent = pick(by_shard, to).astype(jnp.bfloat16)
        panel_grads = panel_grads + lax.ppermute(sent, "blk", pattern).astype(jnp.float32)

    losses = loss.astype(jnp.bfloat16)
    back_l = jnp.zeros((nq // per, per, rows), jnp.bfloat16)
    back_q = jnp.zeros((nq // per, per, rows, width), jnp.bfloat16)
    back_l = lax.dynamic_update_index_in_dim(back_l, losses[:per], mine, 0)
    back_q = lax.dynamic_update_index_in_dim(back_q, jnp.stack(query_grads[:per]), mine, 0)
    for n, (to, source, pattern) in enumerate(group_peers):
        at = slice((n + 1) * per, (n + 2) * per)
        home = [(d, s) for s, d in pattern]
        back_l = lax.dynamic_update_index_in_dim(
            back_l, lax.ppermute(losses[at], "group", home), to, 0
        )
        back_q = lax.dynamic_update_index_in_dim(
            back_q, lax.ppermute(jnp.stack(query_grads[at]), "group", home), to, 0
        )
    return back_l.reshape(nq, rows), back_q.reshape(nq, rows, width), panel_grads


def solution(mesh):
    return jax.shard_map(
        shards,
        mesh=mesh,
        in_specs=(
            P(("tower", "group", "blk"), None, None),
            P(("tower", "group", "blk"), None),
            P(("tower", "group", "blk"), None),
            P("group", None),
            P(("group", "blk"), None, None),
            P(("group", "blk"), None),
        ),
        out_specs=(
            P(("tower", "group", "blk"), None),
            P(("tower", "group", "blk"), None, None),
            P(("group", "blk"), "tower", None),
        ),
        check_vma=False,
    )
```

```python
import functools

import jax
import jax.numpy as jnp
from jax import lax
from jax.experimental import pallas as pl
from jax.experimental.pallas import tpu as pltpu
from jax.sharding import PartitionSpec as P

VMEM_LIMIT = 40 * 1024 * 1024
LANES = 128
TILE = 16
STEP = 64


def peers(axis):
    n = lax.axis_size(axis)
    me = lax.axis_index(axis)
    if n & (n - 1) == 0:
        return [(me ^ k, me ^ k, [(i, i ^ k) for i in range(n)]) for k in range(1, n)]
    return [
        (lax.rem(me + k, n), lax.rem(me + n - k, n), [(i, (i + k) % n) for i in range(n)])
        for k in range(1, n)
    ]


def pick(array, index):
    return lax.dynamic_index_in_dim(array, index, 0, keepdims=False)


def panel_message_kernel(part_rows, panels, scales, out, sem):
    start = pl.multiple_of(lax.axis_index("tower") * part_rows, TILE)
    copy = pltpu.make_async_copy(
        panels.at[pl.ds(start, part_rows), :], out.at[0:part_rows, :], sem
    )
    copy.start()
    items, shard = scales.shape
    out[part_rows : part_rows + items, :] = jnp.zeros((items, out.shape[1]), out.dtype)
    out[part_rows : part_rows + items, 0:shard] = scales[...]
    copy.wait()


def query_message_kernel(per, items, targets, queries, ids, positives, *refs):
    outs, (marks, sems) = refs[:-2], refs[-2:]
    rows = queries.shape[1]
    nsel = ids.shape[1]
    reps = rows // LANES
    goal = targets()
    copies = []
    for n, out in enumerate(outs):
        block = goal[n // per] * per + n % per
        copies.append(
            pltpu.make_async_copy(queries.at[block], out.at[0:rows, :], sems.at[n])
        )
        copies[-1].start()
    for n, out in enumerate(outs):
        block = goal[n // per] * per + n % per
        place = positives[pl.ds(block, 1), :]
        marks[...] = jnp.zeros_like(marks)
        for c in range(reps):
            chunk = place[:, c * LANES : (c + 1) * LANES]
            marks[c : c + 1, 0:LANES] = (chunk // items).astype(jnp.float32)
            marks[c : c + 1, LANES : 2 * LANES] = (chunk % items).astype(jnp.float32)
        marks[reps : reps + 1, 0:nsel] = ids[pl.ds(block, 1), :].astype(jnp.float32)
        out[rows : rows + TILE, :] = marks[...].astype(out.dtype)
    for copy in copies:
        copy.wait()


def score_kernel(dims, *refs):
    nq, nlocal, ntow, n_piece, rows, nsel, items, slots, shard, split = dims
    refs = list(refs)

    def take(n):
        out, refs[:] = refs[:n], refs[n:]
        return out

    meta, pos_local, scale_own, queries, own = take(5)
    messages = take(nq - nlocal)
    pieces = take(n_piece)
    outs = take(nq)
    (keep,) = take(1)
    sends = take(ntow - 1 if split else 0)
    panel, scale, wide, query, score, sel, sel_wide, weight, term, grad, sems = refs
    part = shard // ntow
    cand = nsel * items
    base = nq * nsel
    width = panel.shape[1]
    copies = []

    def fetch(source, target):
        copies.append(pltpu.make_async_copy(source, target, sems.at[len(copies)]))
        copies[-1].start()

    def row(n):
        return pl.multiple_of(meta[base + n] * items, TILE)

    fetch(own, panel.at[pl.ds(row(0), shard * items), :])
    for n, piece in enumerate(pieces):
        fetch(piece.at[0 : part * items, :], panel.at[pl.ds(row(n + 1), part * items), :])
        if n % ntow == 0:
            fetch(
                piece.at[part * items : part * items + items, 0:LANES], scale.at[n // ntow]
            )
    for n, message in enumerate(messages):
        fetch(message, query.at[nlocal + n])
    for n in range(nlocal):
        fetch(queries.at[meta[base + 1 + n_piece] * nlocal + n], query.at[n, 0:rows, :])
    grad[...] = jnp.zeros_like(grad)
    for copy in copies:
        copy.wait()

    item_of = lax.broadcasted_iota(jnp.int32, (shard * items, items), 0) % items
    spread = item_of == lax.broadcasted_iota(jnp.int32, (shard * items, items), 1)
    spread = spread.astype(jnp.bfloat16)

    def widen(values, first):
        lanes = values.shape[1]
        of_item = jnp.dot(spread, values, preferred_element_type=jnp.float32)
        slot_of = lax.broadcasted_iota(jnp.int32, (shard * items, lanes), 0) // items
        mine = slot_of == lax.broadcasted_iota(jnp.int32, (shard * items, lanes), 1)
        wide[pl.ds(first, shard * items), :] = jnp.dot(
            jnp.where(mine, of_item, 0.0).astype(jnp.bfloat16),
            jnp.ones((lanes, LANES), jnp.bfloat16),
            preferred_element_type=jnp.float32,
        )

    widen(scale_own[...], row(0))
    for n in range(n_piece // ntow):
        first = meta[base + 2 + n_piece + n] * (shard * items)
        widen(scale[n], pl.multiple_of(first, TILE))

    reps = rows // LANES
    chunks = cand // STEP

    def gather(b):
        two = b % 2
        for j in range(nsel):
            start = pl.multiple_of(meta[b * nsel + j] * items, TILE)
            at = slice(j * items, (j + 1) * items)
            sel[two, at, :] = panel[pl.ds(start, items), :]
            sel_wide[two, at, :] = wide[pl.ds(start, items), :]
        score[two] = lax.dot_general(
            sel[two],
            query[b, 0:rows, :],
            (((1,), (1,)), ((), ())),
            preferred_element_type=jnp.float32,
        )

    def positions(b):
        if b < nlocal:
            return pos_local[b : b + 1, :]
        marks = query[b, rows : rows + TILE, :].astype(jnp.float32)
        found = [
            marks[n : n + 1, 0:LANES] * items + marks[n : n + 1, LANES : 2 * LANES]
            for n in range(reps)
        ]
        return jnp.concatenate(found, axis=1).astype(jnp.int32)

    gather(0)
    for b in range(nq):
        two = b % 2
        pos = positions(b)
        if b + 1 < nq:
            gather(b + 1)
        peak8 = jnp.full((8, rows), -jnp.inf, jnp.float32)
        for c in range(chunks):
            at = slice(c * STEP, (c + 1) * STEP)
            s = score[two, at, :] * jnp.tile(sel_wide[two, at, :], (1, reps))
            score[two, at, :] = s
            peak8 = jnp.maximum(peak8, jnp.max(s.reshape(STEP // 8, 8, rows), axis=0))
        peak = jnp.max(peak8, axis=0, keepdims=True)
        total8 = jnp.zeros((8, rows), jnp.float32)
        pick8 = jnp.zeros((8, rows), jnp.float32)
        for c in range(chunks):
            at = slice(c * STEP, (c + 1) * STEP)
            s = score[two, at, :]
            hot = lax.broadcasted_iota(jnp.int32, (STEP, rows), 0) == pos - c * STEP
            e = jnp.exp(s - peak)
            score[two, at, :] = e
            total8 = total8 + jnp.sum(e.reshape(STEP // 8, 8, rows), axis=0)
            picked = jnp.where(hot, s, 0.0)
            pick8 = pick8 + jnp.sum(picked.reshape(STEP // 8, 8, rows), axis=0)
        total = jnp.sum(total8, axis=0, keepdims=True)
        loss = peak + jnp.log(total) - jnp.sum(pick8, axis=0, keepdims=True)
        inverse = 1.0 / total
        for c in range(chunks):
            at = slice(c * STEP, (c + 1) * STEP)
            hot = lax.broadcasted_iota(jnp.int32, (STEP, rows), 0) == pos - c * STEP
            chance = score[two, at, :] * inverse - jnp.where(hot, 1.0, 0.0)
            w = chance * jnp.tile(sel_wide[two, at, :], (1, reps))
            weight[two, at, :] = w.astype(jnp.bfloat16)
        term[two] = jnp.dot(
            weight[two], query[b, 0:rows, :], preferred_element_type=jnp.float32
        )
        outs[b][0:rows, :] = lax.dot_general(
            weight[two],
            sel[two],
            (((0,), (0,)), ((), ())),
            preferred_element_type=jnp.float32,
        ).astype(jnp.bfloat16)
        line = lax.broadcasted_iota(jnp.int32, (TILE, LANES), 0)
        below = jnp.zeros((TILE, LANES), jnp.float32)
        for n in range(reps):
            below = jnp.where(line == n, loss[:, n * LANES : (n + 1) * LANES], below)
        outs[b][rows : rows + TILE, :] = jnp.zeros((TILE, width), jnp.bfloat16)
        outs[b][rows : rows + TILE, 0:LANES] = below.astype(jnp.bfloat16)
        for j in range(nsel):
            slot = meta[b * nsel + j]
            add = term[two, j * items : (j + 1) * items, :]
            if split:
                grad[slot] += add.reshape(ntow, items // ntow, width)
            else:
                start = pl.multiple_of(slot * items, TILE)
                grad[pl.ds(start, items), :] += add
    if split:
        own_at = base + 2 + n_piece + n_piece // ntow
        keep[...] = grad[:, meta[own_at]].reshape(keep.shape)
        for n, send in enumerate(sends):
            send[...] = grad[:, meta[own_at + 1 + n]].reshape(send.shape).astype(send.dtype)
    else:
        keep[...] = grad[...]


def shards(queries, cluster_ids, positives, owner_map, panels, scales):
    nq, rows, width = queries.shape
    shard, items = scales.shape
    nsel = cluster_ids.shape[1]
    nblk, ntow = lax.axis_size("blk"), lax.axis_size("tower")
    slots = shard * nblk
    part = shard // ntow
    cand = nsel * items
    ngroup = lax.axis_size("group")
    mine, blk_me, tow_me = lax.axis_index("group"), lax.axis_index("blk"), lax.axis_index("tower")
    group_peers, blk_peers, tow_peers = peers("group"), peers("blk"), peers("tower")
    per = nq // ngroup
    split = (items // ntow) % 8 == 0
    vmem = pl.BlockSpec(memory_space=pltpu.VMEM)
    smem = pl.BlockSpec(memory_space=pltpu.SMEM)
    hbm = pl.BlockSpec(memory_space=pl.ANY)
    params = pltpu.CompilerParams(vmem_limit_bytes=VMEM_LIMIT)
    flat_panels = panels.reshape(shard * items, width)
    flat_scales = scales.T

    message = pl.pallas_call(
        functools.partial(panel_message_kernel, part * items),
        out_shape=jax.ShapeDtypeStruct((part * items + items, width), panels.dtype),
        in_specs=[hbm, vmem],
        out_specs=vmem,
        scratch_shapes=[pltpu.SemaphoreType.DMA],
        compiler_params=params,
        name="panel_message",
    )(flat_panels, flat_scales)
    pieces, firsts, sources = [], [], []
    for to, source, pattern in blk_peers:
        piece = lax.ppermute(message, "blk", pattern)
        pieces.append(piece)
        firsts.append(source * shard + tow_me * part)
        sources.append(source)
        for _, tow_source, tow_pattern in tow_peers:
            pieces.append(lax.ppermute(piece, "tower", tow_pattern))
            firsts.append(source * shard + tow_source * part)

    def targets():
        return [to for to, _, _ in peers("group")]

    leaving = pl.pallas_call(
        functools.partial(query_message_kernel, per, items, targets),
        out_shape=[jax.ShapeDtypeStruct((rows + TILE, width), queries.dtype)] * (nq - per),
        in_specs=[hbm, vmem, vmem],
        out_specs=[vmem] * (nq - per),
        scratch_shapes=[
            pltpu.VMEM((TILE, width), jnp.float32),
            pltpu.SemaphoreType.DMA((nq - per,)),
        ],
        compiler_params=params,
        name="query_message",
    )(queries, cluster_ids, positives)
    arrived = [
        lax.ppermute(leaving[n * per + i], "group", pattern)
        for n, (_, _, pattern) in enumerate(group_peers)
        for i in range(per)
    ]
    reps = rows // LANES
    ids = [pick(cluster_ids.reshape(ngroup, per, nsel), mine)]
    ids += [got[rows + reps : rows + reps + 1, :nsel].astype(jnp.int32) for got in arrived]
    ids = jnp.concatenate(ids, axis=0)
    hot = ids[:, :, None] == lax.iota(jnp.int32, slots)[None, None, :]
    listed = jnp.sum(jnp.where(hot, owner_map[0][None, None, :], 0), axis=2)
    places = [blk_me * shard] + firsts + [mine] + sources
    places += [tow_me] + [to for to, _, _ in tow_peers]
    meta = jnp.concatenate([listed.reshape(-1), jnp.stack(places).astype(jnp.int32)])
    pos_local = pick(positives.reshape(ngroup, per, rows), mine)

    dims = (nq, per, ntow, len(pieces), rows, nsel, items, slots, shard, split)
    sent_rows = slots * items // ntow
    keep_rows = sent_rows if split else slots * items
    n_send = ntow - 1 if split else 0
    grad_shape = (slots, ntow, items // ntow, width) if split else (slots * items, width)
    results = pl.pallas_call(
        functools.partial(score_kernel, dims),
        out_shape=[jax.ShapeDtypeStruct((rows + TILE, width), jnp.bfloat16)] * nq
        + [jax.ShapeDtypeStruct((keep_rows, width), jnp.float32)]
        + [jax.ShapeDtypeStruct((sent_rows, width), jnp.bfloat16)] * n_send,
        in_specs=[smem, vmem, vmem] + [hbm] * (2 + nq - per + len(pieces)),
        out_specs=[vmem] * (nq + 1 + n_send),
        scratch_shapes=[
            pltpu.VMEM((slots * items, width), jnp.bfloat16),
            pltpu.VMEM((max(nblk - 1, 1), items, LANES), jnp.bfloat16),
            pltpu.VMEM((slots * items, LANES), jnp.float32),
            pltpu.VMEM((nq, rows + TILE, width), jnp.bfloat16),
            pltpu.VMEM((2, cand, rows), jnp.float32),
            pltpu.VMEM((2, cand, width), jnp.bfloat16),
            pltpu.VMEM((2, cand, LANES), jnp.float32),
            pltpu.VMEM((2, cand, rows), jnp.bfloat16),
            pltpu.VMEM((2, cand, width), jnp.float32),
            pltpu.VMEM(grad_shape, jnp.float32),
            pltpu.SemaphoreType.DMA((1 + len(pieces) + (nblk - 1) + nq,)),
        ],
        compiler_params=params,
        name="score",
    )(meta, pos_local, flat_scales, queries, flat_panels, *arrived, *pieces)
    query_grads, keep, sends = results[:nq], results[nq], results[nq + 1 :]

    if split:
        total = keep
        for sent, (_, _, pattern) in zip(sends, tow_peers):
            total = total + lax.ppermute(sent, "tower", pattern).astype(jnp.float32)
    else:
        by_part = keep.reshape(slots, ntow, items // ntow, width)
        total = lax.dynamic_index_in_dim(by_part, tow_me, 1, keepdims=False)
        for to, _, pattern in tow_peers:
            sent = lax.dynamic_index_in_dim(by_part, to, 1, keepdims=False)
            sent = sent.astype(jnp.bfloat16)
            total = total + lax.ppermute(sent, "tower", pattern).astype(jnp.float32)
    total, *query_grads = lax.optimization_barrier((total, *query_grads))
    by_shard = total.reshape(nblk, shard, items // ntow, width)
    panel_grads = pick(by_shard, blk_me)
    for to, _, pattern in blk_peers:
        sent = pick(by_shard, to).astype(jnp.bfloat16)
        panel_grads = panel_grads + lax.ppermute(sent, "blk", pattern).astype(jnp.float32)

    back = [(mine, query_grads[:per])]
    for n, (to, _, pattern) in enumerate(group_peers):
        home = [(d, s) for s, d in pattern]
        blocks = query_grads[(n + 1) * per : (n + 2) * per]
        back.append((to, [lax.ppermute(block, "group", home) for block in blocks]))
    back_q = jnp.zeros((nq, rows, width), jnp.bfloat16)
    back_l = jnp.zeros((nq, rows), jnp.bfloat16)
    for to, blocks in back:
        for i, block in enumerate(blocks):
            back_q = lax.dynamic_update_index_in_dim(back_q, block[:rows], to * per + i, 0)
            line = block[rows : rows + reps, :LANES].reshape(rows)
            back_l = lax.dynamic_update_index_in_dim(back_l, line, to * per + i, 0)
    return back_l, back_q, panel_grads


def solution(mesh):
    return jax.shard_map(
        shards,
        mesh=mesh,
        in_specs=(
            P(("tower", "group", "blk"), None, None),
            P(("tower", "group", "blk"), None),
            P(("tower", "group", "blk"), None),
            P("group", None),
            P(("group", "blk"), None, None),
            P(("group", "blk"), None),
        ),
        out_specs=(
            P(("tower", "group", "blk"), None),
            P(("tower", "group", "blk"), None, None),
            P(("group", "blk"), "tower", None),
        ),
        check_vma=False,
    )
```

```python
import functools
import math

import jax
import jax.numpy as jnp
from jax import lax
from jax.experimental import pallas as pl
from jax.experimental.pallas import tpu as pltpu
from jax.sharding import PartitionSpec as P

VMEM_LIMIT = 40 * 1024 * 1024
LANES = 128
TILE = 16
ORDER = (
    (("r", 0), ("g", 0), ("s", 0), ("p", 0), ("r", 1)),
    (("g", 1), ("s", 1), ("e", 0), ("w", 0), ("t", 0), ("p", 1), ("q", 0), ("a", 0)),
    (),
)
LN2 = math.log(2.0)


def peers(axis):
    n = lax.axis_size(axis)
    me = lax.axis_index(axis)
    if n & (n - 1) == 0:
        return [(me ^ k, me ^ k, [(i, i ^ k) for i in range(n)]) for k in range(1, n)]
    return [
        (lax.rem(me + k, n), lax.rem(me + n - k, n), [(i, (i + k) % n) for i in range(n)])
        for k in range(1, n)
    ]


def pick(array, index):
    return lax.dynamic_index_in_dim(array, index, 0, keepdims=False)


def panel_message_kernel(part_rows, panels, scales, out, held, sems):
    start = pl.multiple_of(lax.axis_index("tower") * part_rows, TILE)
    copy = pltpu.make_async_copy(
        panels.at[pl.ds(start, part_rows), :], out.at[0:part_rows, :], sems.at[0]
    )
    copy.start()
    fetch = pltpu.make_async_copy(scales, held, sems.at[1])
    fetch.start()
    items, shard = scales.shape
    out[part_rows : part_rows + items, :] = jnp.zeros((items, out.shape[1]), out.dtype)
    fetch.wait()
    out[part_rows : part_rows + items, 0:shard] = held[...]
    copy.wait()


def query_message_kernel(per, items, targets, queries, ids_far, positives_far, *refs):
    (*outs, ids, positives, marks, sems) = refs
    rows = queries.shape[1]
    nsel = ids.shape[1]
    reps = rows // LANES
    goal = targets()
    lists = [
        pltpu.make_async_copy(ids_far, ids, sems.at[len(outs)]),
        pltpu.make_async_copy(positives_far, positives, sems.at[len(outs) + 1]),
    ]
    for copy in lists:
        copy.start()
    copies = []
    for n, out in enumerate(outs):
        block = goal[n // per] * per + n % per
        copies.append(
            pltpu.make_async_copy(queries.at[block], out.at[0:rows, :], sems.at[n])
        )
        copies[-1].start()
    for copy in lists:
        copy.wait()
    for n, out in enumerate(outs):
        block = goal[n // per] * per + n % per
        place = positives[pl.ds(block, 1), :]
        marks[...] = jnp.zeros_like(marks)
        for c in range(reps):
            chunk = place[:, c * LANES : (c + 1) * LANES]
            marks[c : c + 1, 0:LANES] = (chunk // items).astype(jnp.float32)
            marks[c : c + 1, LANES : 2 * LANES] = (chunk % items).astype(jnp.float32)
        marks[reps : reps + 1, 0:nsel] = ids[pl.ds(block, 1), :].astype(jnp.float32)
        out[rows : rows + TILE, :] = marks[...].astype(out.dtype)
    for copy in copies:
        copy.wait()


def score_kernel(dims, *refs):
    nq, nlocal, ntow, n_piece, rows, nsel, items, slots, shard, split = dims
    refs = list(refs)

    def take(n):
        out, refs[:] = refs[:n], refs[n:]
        return out

    owner_far, ids_far, pos_far, scale_far, queries, own = take(6)
    messages = take(nq - nlocal)
    pieces = take(n_piece)
    outs = take(nq)
    (keep,) = take(1)
    sends = take(ntow - 1 if split else 0)
    (panel, scale, wide, query, score, sel, sel_wide, weight, term, back, grad, place) = refs[:12]
    (owner, ids, far_ids, moved_ids, pos_own, scale_own, sems) = refs[12:]
    part = shard // ntow
    cand = nsel * items
    width = panel.shape[1]
    mine, blk_me, tow_me = lax.axis_index("group"), lax.axis_index("blk"), lax.axis_index("tower")
    blk_to = [to for _, to, _ in peers("blk")]
    tow_to = [to for _, to, _ in peers("tower")]
    copies = []

    def fetch(source, target):
        copies.append(pltpu.make_async_copy(source, target, sems.at[len(copies)]))
        copies[-1].start()
        return copies[-1]

    def rows_at(slot, count):
        return pl.ds(pl.multiple_of(slot * items, TILE), count * items)

    early = [fetch(ids_far, ids), fetch(owner_far, owner)]
    early.append(fetch(scale_far, scale_own))
    early.append(fetch(pos_far, pos_own))
    early.append(fetch(own, panel.at[rows_at(blk_me * shard, shard), :]))
    for n, piece in enumerate(pieces):
        first = blk_to[n // ntow] * shard + ([tow_me] + tow_to)[n % ntow] * part
        held = piece.at[0 : part * items, :]
        early.append(fetch(held, panel.at[rows_at(first, part), :]))
        if n % ntow == 0:
            held = piece.at[part * items : part * items + items, 0:LANES]
            early.append(fetch(held, scale.at[n // ntow]))
    blocks = []
    for n in range(nlocal):
        blocks.append(fetch(queries.at[mine * nlocal + n], query.at[n, 0:rows, :]))
    for n, message in enumerate(messages):
        blocks.append(fetch(message, query.at[nlocal + n]))
    grad[...] = jnp.zeros_like(grad)
    for copy in early:
        copy.wait()

    reps = rows // LANES
    moved = []

    def arrive(b):
        blocks[b].wait()
        if b < nlocal:
            place[b] = jnp.broadcast_to(pos_own[pl.ds(mine * nlocal + b, 1), :], (8, rows))
            return
        marks = query[b, rows : rows + TILE, :].astype(jnp.float32)
        found = [
            marks[n : n + 1, 0:LANES] * items + marks[n : n + 1, LANES : 2 * LANES]
            for n in range(reps)
        ]
        found = jnp.concatenate(found, axis=1).astype(jnp.int32)
        place[b] = jnp.broadcast_to(found, (8, rows))
        moved_ids[b] = jnp.broadcast_to(marks[reps : reps + 1, 0:LANES], (8, LANES)).astype(
            jnp.int32
        )
        moved.append(fetch(moved_ids.at[b], far_ids.at[b]))

    def slot_of(b, j):
        if b < nlocal:
            return owner[0, ids[mine * nlocal + b, j]]
        return owner[0, far_ids[b, 0, j]]

    item_of = lax.broadcasted_iota(jnp.int32, (shard * items, items), 0) % items
    spread = item_of == lax.broadcasted_iota(jnp.int32, (shard * items, items), 1)
    spread = spread.astype(jnp.bfloat16)

    def widen(values, at):
        lanes = values.shape[1]
        of_item = jnp.dot(spread, values, preferred_element_type=jnp.float32)
        slot_of = lax.broadcasted_iota(jnp.int32, (shard * items, lanes), 0) // items
        mine = slot_of == lax.broadcasted_iota(jnp.int32, (shard * items, lanes), 1)
        wide[at, :] = jnp.dot(
            jnp.where(mine, of_item, 0.0).astype(jnp.bfloat16),
            jnp.ones((lanes, LANES), jnp.bfloat16),
            preferred_element_type=jnp.float32,
        ) * (1.0 / LN2)

    widen(scale_own[...], rows_at(blk_me * shard, shard))
    for n, to in enumerate(blk_to):
        widen(scale[n], rows_at(to * shard, shard))

    line = lax.broadcasted_iota(jnp.int32, (8, rows), 0)
    state = [{} for _ in range(nq)]

    def gather(b):
        two = b % 2
        for j in range(nsel):
            at = slice(j * items, (j + 1) * items)
            slot = rows_at(slot_of(b, j), 1)
            sel[two, at, :] = panel[slot, :]
            sel_wide[two, at, :] = wide[slot, :]

    def scores(b):
        score[b % 2] = lax.dot_general(
            sel[b % 2],
            query[b, 0:rows, :],
            (((1,), (1,)), ((), ())),
            preferred_element_type=jnp.float32,
        )

    def spread_scale(two, first):
        return jnp.tile(sel_wide[two, first : first + 8, :], (1, reps))

    def peaks(b):
        two = b % 2
        peak = jnp.full((8, rows), -jnp.inf, jnp.float32)
        for first in range(0, cand, 8):
            s = score[two, first : first + 8, :] * spread_scale(two, first)
            score[two, first : first + 8, :] = s
            peak = jnp.maximum(peak, s)
        state[b]["top"] = jnp.max(peak, axis=0, keepdims=True)

    def exps(b):
        two, top, pos = b % 2, state[b]["top"], place[b]
        total = jnp.zeros((8, rows), jnp.float32)
        pick = jnp.zeros((8, rows), jnp.float32)
        for first in range(0, cand, 8):
            s = score[two, first : first + 8, :]
            e = jnp.exp2(s - top)
            score[two, first : first + 8, :] = e
            total = total + e
            pick = jnp.where(line == pos - first, s, pick)
        total = jnp.sum(total, axis=0, keepdims=True)
        picked = jnp.sum(pick, axis=0, keepdims=True)
        loss = (top - picked) * LN2 + jnp.log(total)
        state[b]["inverse"] = LN2 / total
        row_of = lax.broadcasted_iota(jnp.int32, (TILE, LANES), 0)
        below = jnp.zeros((TILE, LANES), jnp.float32)
        for n in range(reps):
            below = jnp.where(row_of == n, loss[:, n * LANES : (n + 1) * LANES], below)
        back[b, rows : rows + TILE, :] = jnp.zeros((TILE, width), jnp.bfloat16)
        back[b, rows : rows + TILE, 0:LANES] = below.astype(jnp.bfloat16)

    def weigh(b):
        two, inverse, pos = b % 2, state[b]["inverse"], place[b]
        for start in range(0, cand, TILE):
            halves = []
            for first in range(start, start + TILE, 8):
                chance = score[two, first : first + 8, :] * inverse
                chance = jnp.where(line == pos - first, chance - LN2, chance)
                halves.append(chance * spread_scale(two, first))
            weight[two, start : start + TILE, :] = jnp.concatenate(halves, axis=0).astype(
                jnp.bfloat16
            )

    def panel_terms(b):
        term[b % 2] = jnp.dot(
            weight[b % 2], query[b, 0:rows, :], preferred_element_type=jnp.float32
        )

    def scatter(b):
        for j in range(nsel):
            slot = slot_of(b, j)
            add = term[b % 2, j * items : (j + 1) * items, :]
            if split:
                grad[slot] += add.reshape(ntow, items // ntow, width)
            else:
                grad[rows_at(slot, 1), :] += add

    def query_terms(b):
        back[b, 0:rows, :] = lax.dot_general(
            weight[b % 2],
            sel[b % 2],
            (((0,), (0,)), ((), ())),
            preferred_element_type=jnp.float32,
        ).astype(jnp.bfloat16)
        leaves.append(pltpu.make_async_copy(back.at[b], outs[b], sems.at[sems.shape[0] - nq + b]))
        leaves[-1].start()

    leaves = []
    def ready(b):
        if b == 0:
            arrive(0)
        if b == 1:
            for n in range(1, nq):
                arrive(n)
            for copy in moved:
                copy.wait()

    jobs = dict(r=ready, g=gather, s=scores, p=peaks, e=exps, w=weigh, t=panel_terms, a=scatter, q=query_terms)
    for name, shift in ORDER[0]:
        if shift < nq:
            jobs[name](shift)
    for b in range(nq):
        for name, shift in ORDER[1]:
            if 0 <= b + shift < nq:
                jobs[name](b + shift)
    for name, shift in ORDER[2]:
        jobs[name](nq - 1 + shift)
    if split:
        keep[...] = grad[:, tow_me].reshape(keep.shape)
        for to, send in zip([to for to, _, _ in peers("tower")], sends):
            send[...] = grad[:, to].reshape(send.shape).astype(send.dtype)
    else:
        keep[...] = grad[...]
    for copy in leaves:
        copy.wait()


def tower_sum_kernel(nblk, partners, keep, *refs):
    got, outs = refs[: len(refs) - nblk], refs[len(refs) - nblk :]
    me, to = partners()
    rows = keep.shape[0] // nblk
    for owner, out in zip([me] + to, outs):
        at = pl.ds(pl.multiple_of(owner * rows, TILE), rows)
        total = keep[at, :]
        for term in got:
            total = total + term[at, :].astype(jnp.float32)
        out[...] = total.astype(out.dtype)


def shard_sum_kernel(own, *refs):
    total = own[...]
    for term in refs[:-1]:
        total = total + term[...].astype(jnp.float32)
    refs[-1][...] = total


def home_kernel(per, partners, *refs):
    (*blocks, grads, losses, sems) = refs
    nq, rows, _ = grads.shape
    me, to = partners()
    copies = []
    lines = lax.broadcasted_iota(jnp.int32, (nq, LANES), 0)
    parts = [jnp.zeros((nq, LANES), jnp.float32)] * (rows // LANES)
    for n, block in enumerate(blocks):
        place = ([me] + to)[n // per] * per + n % per
        copies.append(
            pltpu.make_async_copy(block.at[0:rows, :], grads.at[place], sems.at[n])
        )
        copies[-1].start()
    for n, block in enumerate(blocks):
        place = ([me] + to)[n // per] * per + n % per
        tile = block[rows : rows + TILE, 0:LANES].astype(jnp.float32)
        parts = [jnp.where(lines == place, tile[c : c + 1, :], p) for c, p in enumerate(parts)]
    losses[...] = jnp.concatenate(parts, axis=1).astype(losses.dtype)
    for copy in copies:
        copy.wait()


def shards(queries, cluster_ids, positives, owner_map, panels, scales):
    nq, rows, width = queries.shape
    shard, items = scales.shape
    nsel = cluster_ids.shape[1]
    nblk, ntow = lax.axis_size("blk"), lax.axis_size("tower")
    slots = shard * nblk
    part = shard // ntow
    cand = nsel * items
    ngroup = lax.axis_size("group")
    mine, blk_me, tow_me = lax.axis_index("group"), lax.axis_index("blk"), lax.axis_index("tower")
    group_peers, blk_peers, tow_peers = peers("group"), peers("blk"), peers("tower")
    per = nq // ngroup
    split = (items // ntow) % 8 == 0
    vmem = pl.BlockSpec(memory_space=pltpu.VMEM)
    hbm = pl.BlockSpec(memory_space=pltpu.HBM)
    where = pl.BlockSpec(memory_space=pl.ANY)
    pin = functools.partial(pltpu.with_memory_space_constraint, memory_space=pltpu.HBM)
    params = pltpu.CompilerParams(vmem_limit_bytes=VMEM_LIMIT)
    flat_panels = panels.reshape(shard * items, width)
    flat_scales = scales.T

    message = pl.pallas_call(
        functools.partial(panel_message_kernel, part * items),
        out_shape=jax.ShapeDtypeStruct((part * items + items, width), panels.dtype),
        in_specs=[hbm, hbm],
        out_specs=vmem,
        scratch_shapes=[
            pltpu.VMEM((items, shard), scales.dtype),
            pltpu.SemaphoreType.DMA((2,)),
        ],
        compiler_params=params,
        name="panel_message",
    )(pin(flat_panels), pin(flat_scales))
    pieces = []
    for to, source, pattern in blk_peers:
        piece = lax.ppermute(message, "blk", pattern)
        pieces.append(piece)
        for _, tow_source, tow_pattern in tow_peers:
            pieces.append(lax.ppermute(piece, "tower", tow_pattern))

    def targets():
        return [to for to, _, _ in peers("group")]

    leaving = pl.pallas_call(
        functools.partial(query_message_kernel, per, items, targets),
        out_shape=[jax.ShapeDtypeStruct((rows + TILE, width), queries.dtype)] * (nq - per),
        in_specs=[hbm, hbm, hbm],
        out_specs=[vmem] * (nq - per),
        scratch_shapes=[
            pltpu.VMEM(cluster_ids.shape, jnp.int32),
            pltpu.VMEM(positives.shape, jnp.int32),
            pltpu.VMEM((TILE, width), jnp.float32),
            pltpu.SemaphoreType.DMA((nq - per + 2,)),
        ],
        compiler_params=params,
        name="query_message",
    )(pin(queries), pin(cluster_ids), pin(positives))
    arrived = [
        lax.ppermute(leaving[n * per + i], "group", pattern)
        for n, (_, _, pattern) in enumerate(group_peers)
        for i in range(per)
    ]
    dims = (nq, per, ntow, len(pieces), rows, nsel, items, slots, shard, split)
    sent_rows = slots * items // ntow
    keep_rows = sent_rows if split else slots * items
    n_send = ntow - 1 if split else 0
    grad_shape = (slots, ntow, items // ntow, width) if split else (slots * items, width)
    results = pl.pallas_call(
        functools.partial(score_kernel, dims),
        out_shape=[pltpu.HBM((rows + TILE, width), jnp.bfloat16)] * nq
        + [pltpu.VMEM((keep_rows, width), jnp.float32)]
        + [pltpu.VMEM((sent_rows, width), jnp.bfloat16)] * n_send,
        in_specs=[hbm] * 6 + [where] * (nq - per + len(pieces)),
        out_specs=[hbm] * nq + [vmem] * (1 + n_send),
        scratch_shapes=[
            pltpu.VMEM((slots * items, width), jnp.bfloat16),
            pltpu.VMEM((max(nblk - 1, 1), items, LANES), jnp.bfloat16),
            pltpu.VMEM((slots * items, LANES), jnp.float32),
            pltpu.VMEM((nq, rows + TILE, width), jnp.bfloat16),
            pltpu.VMEM((2, cand, rows), jnp.float32),
            pltpu.VMEM((2, cand, width), jnp.bfloat16),
            pltpu.VMEM((2, cand, LANES), jnp.float32),
            pltpu.VMEM((2, cand, rows), jnp.bfloat16),
            pltpu.VMEM((2, cand, width), jnp.float32),
            pltpu.VMEM((nq, rows + TILE, width), jnp.bfloat16),
            pltpu.VMEM(grad_shape, jnp.float32),
            pltpu.VMEM((nq, 8, rows), jnp.int32),
            pltpu.SMEM(owner_map.shape, jnp.int32),
            pltpu.SMEM(cluster_ids.shape, jnp.int32),
            pltpu.SMEM((nq, 8, LANES), jnp.int32),
            pltpu.VMEM((nq, 8, LANES), jnp.int32),
            pltpu.VMEM(positives.shape, jnp.int32),
            pltpu.VMEM(flat_scales.shape, flat_scales.dtype),
            pltpu.SemaphoreType.DMA((5 + len(pieces) + (nblk - 1) + 3 * nq,)),
        ],
        compiler_params=params,
        name="score",
    )(
        pin(owner_map),
        pin(cluster_ids),
        pin(positives),
        pin(flat_scales),
        pin(queries),
        pin(flat_panels),
        *arrived,
        *pieces,
    )
    query_grads, keep, sends = results[:nq], results[nq], results[nq + 1 :]

    def partners(axis):
        return lax.axis_index(axis), [to for to, _, _ in peers(axis)]

    shard_rows = shard * items // ntow
    if split:
        got = [lax.ppermute(sent, "tower", p) for sent, (_, _, p) in zip(sends, tow_peers)]
        own, *leaving = pl.pallas_call(
            functools.partial(tower_sum_kernel, nblk, functools.partial(partners, "blk")),
            out_shape=[pltpu.VMEM((shard_rows, width), jnp.float32)]
            + [pltpu.VMEM((shard_rows, width), jnp.bfloat16)] * (nblk - 1),
            in_specs=[vmem] * (1 + len(got)),
            out_specs=[vmem] * nblk,
            compiler_params=params,
            name="tower_sum",
        )(keep, *got)
    else:
        by_part = keep.reshape(slots, ntow, items // ntow, width)
        total = lax.dynamic_index_in_dim(by_part, tow_me, 1, keepdims=False)
        for to, _, pattern in tow_peers:
            sent = lax.dynamic_index_in_dim(by_part, to, 1, keepdims=False)
            sent = sent.astype(jnp.bfloat16)
            total = total + lax.ppermute(sent, "tower", pattern).astype(jnp.float32)
        total = total.reshape(nblk, shard_rows, width)
        own = pick(total, blk_me)
        leaving = [pick(total, to).astype(jnp.bfloat16) for to, _, _ in blk_peers]
    own, *rest = lax.optimization_barrier((own, *leaving, *query_grads))
    leaving, query_grads = rest[: nblk - 1], rest[nblk - 1 :]
    terms = [lax.ppermute(sent, "blk", p) for sent, (_, _, p) in zip(leaving, blk_peers)]
    panel_grads = pl.pallas_call(
        shard_sum_kernel,
        out_shape=jax.ShapeDtypeStruct((shard_rows, width), jnp.float32),
        in_specs=[vmem] * nblk,
        out_specs=vmem,
        compiler_params=params,
        cost_estimate=pl.CostEstimate(flops=10**9, bytes_accessed=10**7, transcendentals=0),
        name="shard_sum",
    )(own, *terms).reshape(shard, items // ntow, width)

    blocks = list(query_grads[:per])
    for n, (to, _, pattern) in enumerate(group_peers):
        home = [(d, s) for s, d in pattern]
        for block in query_grads[(n + 1) * per : (n + 2) * per]:
            blocks.append(lax.ppermute(block, "group", home))
    back_q, back_l = pl.pallas_call(
        functools.partial(home_kernel, per, functools.partial(partners, "group")),
        out_shape=[
            pltpu.HBM((nq, rows, width), jnp.bfloat16),
            jax.ShapeDtypeStruct((nq, rows), jnp.bfloat16),
        ],
        in_specs=[vmem] * nq,
        out_specs=[hbm, vmem],
        scratch_shapes=[pltpu.SemaphoreType.DMA((nq,))],
        compiler_params=params,
        name="home",
    )(*blocks)
    return back_l, back_q, panel_grads


def solution(mesh):
    return jax.shard_map(
        shards,
        mesh=mesh,
        in_specs=(
            P(("tower", "group", "blk"), None, None),
            P(("tower", "group", "blk"), None),
            P(("tower", "group", "blk"), None),
            P("group", None),
            P(("group", "blk"), None, None),
            P(("group", "blk"), None),
        ),
        out_specs=(
            P(("tower", "group", "blk"), None),
            P(("tower", "group", "blk"), None, None),
            P(("group", "blk"), "tower", None),
        ),
        check_vma=False,
    )
```

```python
import functools
import math

import jax
import jax.numpy as jnp
from jax import lax
from jax.experimental import pallas as pl
from jax.experimental.pallas import tpu as pltpu
from jax.sharding import PartitionSpec as P

VMEM_LIMIT = 40 * 1024 * 1024
LANES = 128
TILE = 16
ORDER = (
    (("g", 0), ("s", 0), ("p", 0)),
    (("g", 1), ("s", 1), ("e", 0), ("w", 0), ("t", 0), ("p", 1), ("q", 0), ("a", 0)),
    (),
)
LN2 = math.log(2.0)


def peers(axis):
    n = lax.axis_size(axis)
    me = lax.axis_index(axis)
    if n & (n - 1) == 0:
        return [(me ^ k, me ^ k, [(i, i ^ k) for i in range(n)]) for k in range(1, n)]
    return [
        (lax.rem(me + k, n), lax.rem(me + n - k, n), [(i, (i + k) % n) for i in range(n)])
        for k in range(1, n)
    ]


def pick(array, index):
    return lax.dynamic_index_in_dim(array, index, 0, keepdims=False)


def panel_message_kernel(part_rows, panels, scales, out, held, sems):
    start = pl.multiple_of(lax.axis_index("tower") * part_rows, TILE)
    copy = pltpu.make_async_copy(
        panels.at[pl.ds(start, part_rows), :], out.at[0:part_rows, :], sems.at[0]
    )
    copy.start()
    fetch = pltpu.make_async_copy(scales, held, sems.at[1])
    fetch.start()
    items, shard = scales.shape
    out[part_rows : part_rows + items, :] = jnp.zeros((items, out.shape[1]), out.dtype)
    fetch.wait()
    out[part_rows : part_rows + items, 0:shard] = held[...]
    copy.wait()


def query_message_kernel(per, items, targets, queries, ids_far, positives_far, *refs):
    (*outs, ids, positives, marks, sems) = refs
    rows = queries.shape[1]
    nsel = ids.shape[1]
    reps = rows // LANES
    goal = targets()
    lists = [
        pltpu.make_async_copy(ids_far, ids, sems.at[len(outs)]),
        pltpu.make_async_copy(positives_far, positives, sems.at[len(outs) + 1]),
    ]
    for copy in lists:
        copy.start()
    copies = []
    for n, out in enumerate(outs):
        block = goal[n // per] * per + n % per
        copies.append(
            pltpu.make_async_copy(queries.at[block], out.at[0:rows, :], sems.at[n])
        )
        copies[-1].start()
    for copy in lists:
        copy.wait()
    for n, out in enumerate(outs):
        block = goal[n // per] * per + n % per
        place = positives[pl.ds(block, 1), :]
        marks[...] = jnp.zeros_like(marks)
        for c in range(reps):
            chunk = place[:, c * LANES : (c + 1) * LANES]
            marks[c : c + 1, 0:LANES] = (chunk // items).astype(jnp.float32)
            marks[c : c + 1, LANES : 2 * LANES] = (chunk % items).astype(jnp.float32)
        marks[reps : reps + 1, 0:nsel] = ids[pl.ds(block, 1), :].astype(jnp.float32)
        out[rows : rows + TILE, :] = marks[...].astype(out.dtype)
    for copy in copies:
        copy.wait()


def score_kernel(dims, *refs):
    nq, nlocal, ntow, n_piece, rows, nsel, items, slots, shard, split = dims
    refs = list(refs)

    def take(n):
        out, refs[:] = refs[:n], refs[n:]
        return out

    owner_far, ids_far, pos_far, scale_far, queries, own = take(6)
    messages = take(nq - nlocal)
    pieces = take(n_piece)
    outs = take(nq)
    (keep,) = take(1)
    sends = take(ntow - 1 if split else 0)
    (panel, wide, query, score, sel, sel_wide, weight, term, grad, place) = refs[:10]
    (owner, ids, far_ids, moved_ids, pos_own, scale_own, sems) = refs[10:]
    part = shard // ntow
    cand = nsel * items
    width = panel.shape[1]
    mine, blk_me, tow_me = lax.axis_index("group"), lax.axis_index("blk"), lax.axis_index("tower")
    blk_to = [to for _, to, _ in peers("blk")]
    tow_to = [to for _, to, _ in peers("tower")]
    copies = []

    def fetch(source, target):
        copies.append(pltpu.make_async_copy(source, target, sems.at[len(copies)]))
        copies[-1].start()
        return copies[-1]

    def rows_at(slot, count):
        return pl.ds(pl.multiple_of(slot * items, TILE), count * items)

    early = [fetch(ids_far, ids), fetch(owner_far, owner)]
    early.append(fetch(scale_far, scale_own))
    early.append(fetch(pos_far, pos_own))
    early.append(fetch(own, panel.at[rows_at(blk_me * shard, shard), :]))
    local = [fetch(queries.at[mine * nlocal + n], query.at[n]) for n in range(nlocal)]
    for n, piece in enumerate(pieces):
        first = blk_to[n // ntow] * shard + ([tow_me] + tow_to)[n % ntow] * part
        panel[rows_at(first, part), :] = piece[0 : part * items, :]
    grad[...] = jnp.zeros_like(grad)

    def block_rows(b):
        return query[b] if b < nlocal else messages[b - nlocal][0:rows, :]

    reps = rows // LANES
    moved = []

    for b in range(nlocal, nq):
        marks = messages[b - nlocal][rows : rows + TILE, :].astype(jnp.float32)
        found = [
            marks[n : n + 1, 0:LANES] * items + marks[n : n + 1, LANES : 2 * LANES]
            for n in range(reps)
        ]
        found = jnp.concatenate(found, axis=1).astype(jnp.int32)
        place[b] = jnp.broadcast_to(found, (8, rows))
        far = jnp.broadcast_to(marks[reps : reps + 1, 0:LANES], (8, LANES))
        moved_ids[b] = far.astype(jnp.int32)
        moved.append(fetch(moved_ids.at[b], far_ids.at[b]))
    for copy in early + local + moved:
        copy.wait()
    for b in range(nlocal):
        place[b] = jnp.broadcast_to(pos_own[pl.ds(mine * nlocal + b, 1), :], (8, rows))

    def slot_of(b, j):
        if b < nlocal:
            return owner[0, ids[mine * nlocal + b, j]]
        return owner[0, far_ids[b, 0, j]]

    item_of = lax.broadcasted_iota(jnp.int32, (shard * items, items), 0) % items
    spread = item_of == lax.broadcasted_iota(jnp.int32, (shard * items, items), 1)
    spread = spread.astype(jnp.bfloat16)

    def widen(values, at):
        lanes = values.shape[1]
        of_item = jnp.dot(spread, values, preferred_element_type=jnp.float32)
        slot_of = lax.broadcasted_iota(jnp.int32, (shard * items, lanes), 0) // items
        mine = slot_of == lax.broadcasted_iota(jnp.int32, (shard * items, lanes), 1)
        wide[at, :] = jnp.dot(
            jnp.where(mine, of_item, 0.0).astype(jnp.bfloat16),
            jnp.ones((lanes, LANES), jnp.bfloat16),
            preferred_element_type=jnp.float32,
        ) * (1.0 / LN2)

    widen(scale_own[...], rows_at(blk_me * shard, shard))
    for n, to in enumerate(blk_to):
        widen(pieces[n * ntow][part * items : part * items + items, 0:LANES], rows_at(to * shard, shard))

    line = lax.broadcasted_iota(jnp.int32, (8, rows), 0)
    state = [{} for _ in range(nq)]

    def gather(b):
        two = b % 2
        for j in range(nsel):
            at = slice(j * items, (j + 1) * items)
            slot = rows_at(slot_of(b, j), 1)
            sel[two, at, :] = panel[slot, :]
            sel_wide[two, at, :] = wide[slot, :]

    def scores(b):
        score[b % 2] = lax.dot_general(
            sel[b % 2],
            block_rows(b),
            (((1,), (1,)), ((), ())),
            preferred_element_type=jnp.float32,
        )

    def spread_scale(two, first):
        return jnp.tile(sel_wide[two, first : first + 8, :], (1, reps))

    def peaks(b):
        two = b % 2
        peak = jnp.full((8, rows), -jnp.inf, jnp.float32)
        for first in range(0, cand, 8):
            s = score[two, first : first + 8, :] * spread_scale(two, first)
            score[two, first : first + 8, :] = s
            peak = jnp.maximum(peak, s)
        state[b]["top"] = jnp.max(peak, axis=0, keepdims=True)

    def exps(b):
        two, top, pos = b % 2, state[b]["top"], place[b]
        total = jnp.zeros((8, rows), jnp.float32)
        pick = jnp.zeros((8, rows), jnp.float32)
        for first in range(0, cand, 8):
            s = score[two, first : first + 8, :]
            e = jnp.exp2(s - top)
            score[two, first : first + 8, :] = e
            total = total + e
            pick = jnp.where(line == pos - first, s, pick)
        total = jnp.sum(total, axis=0, keepdims=True)
        picked = jnp.sum(pick, axis=0, keepdims=True)
        loss = (top - picked) * LN2 + jnp.log(total)
        state[b]["inverse"] = LN2 / total
        row_of = lax.broadcasted_iota(jnp.int32, (TILE, LANES), 0)
        below = jnp.zeros((TILE, LANES), jnp.float32)
        for n in range(reps):
            below = jnp.where(row_of == n, loss[:, n * LANES : (n + 1) * LANES], below)
        outs[b][rows : rows + TILE, :] = jnp.zeros((TILE, width), jnp.bfloat16)
        outs[b][rows : rows + TILE, 0:LANES] = below.astype(jnp.bfloat16)

    def weigh(b):
        two, inverse, pos = b % 2, state[b]["inverse"], place[b]
        for start in range(0, cand, TILE):
            halves = []
            for first in range(start, start + TILE, 8):
                chance = score[two, first : first + 8, :] * inverse
                chance = jnp.where(line == pos - first, chance - LN2, chance)
                halves.append(chance * spread_scale(two, first))
            weight[two, start : start + TILE, :] = jnp.concatenate(halves, axis=0).astype(
                jnp.bfloat16
            )

    def panel_terms(b):
        term[b % 2] = jnp.dot(
            weight[b % 2], block_rows(b), preferred_element_type=jnp.float32
        )

    def scatter(b):
        for j in range(nsel):
            slot = slot_of(b, j)
            add = term[b % 2, j * items : (j + 1) * items, :]
            if split:
                grad[slot] += add.reshape(ntow, items // ntow, width)
            else:
                grad[rows_at(slot, 1), :] += add

    def query_terms(b):
        outs[b][0:rows, :] = lax.dot_general(
            weight[b % 2],
            sel[b % 2],
            (((0,), (0,)), ((), ())),
            preferred_element_type=jnp.float32,
        ).astype(jnp.bfloat16)

    jobs = dict(g=gather, s=scores, p=peaks, e=exps, w=weigh, t=panel_terms, a=scatter, q=query_terms)
    for name, shift in ORDER[0]:
        if shift < nq:
            jobs[name](shift)
    for b in range(nq):
        for name, shift in ORDER[1]:
            if 0 <= b + shift < nq:
                jobs[name](b + shift)
    for name, shift in ORDER[2]:
        jobs[name](nq - 1 + shift)
    if split:
        keep[...] = grad[:, tow_me].reshape(keep.shape)
        for to, send in zip([to for to, _, _ in peers("tower")], sends):
            send[...] = grad[:, to].reshape(send.shape).astype(send.dtype)
    else:
        keep[...] = grad[...]


def tower_sum_kernel(nblk, partners, keep, *refs):
    got, outs = refs[: len(refs) - nblk], refs[len(refs) - nblk :]
    me, to = partners()
    rows = keep.shape[0] // nblk
    for owner, out in zip([me] + to, outs):
        at = pl.ds(pl.multiple_of(owner * rows, TILE), rows)
        total = keep[at, :]
        for term in got:
            total = total + term[at, :].astype(jnp.float32)
        out[...] = total.astype(out.dtype)


def shard_sum_kernel(own, *refs):
    total = own[...]
    for term in refs[:-1]:
        total = total + term[...].astype(jnp.float32)
    refs[-1][...] = total


def home_kernel(per, partners, *refs):
    (*blocks, grads, losses, sems) = refs
    nq, rows, _ = grads.shape
    me, to = partners()
    copies = []
    lines = lax.broadcasted_iota(jnp.int32, (nq, LANES), 0)
    parts = [jnp.zeros((nq, LANES), jnp.float32)] * (rows // LANES)
    for n, block in enumerate(blocks):
        place = ([me] + to)[n // per] * per + n % per
        copies.append(
            pltpu.make_async_copy(block.at[0:rows, :], grads.at[place], sems.at[n])
        )
        copies[-1].start()
    for n, block in enumerate(blocks):
        place = ([me] + to)[n // per] * per + n % per
        tile = block[rows : rows + TILE, 0:LANES].astype(jnp.float32)
        parts = [jnp.where(lines == place, tile[c : c + 1, :], p) for c, p in enumerate(parts)]
    losses[...] = jnp.concatenate(parts, axis=1).astype(losses.dtype)
    for copy in copies:
        copy.wait()


def shards(queries, cluster_ids, positives, owner_map, panels, scales):
    nq, rows, width = queries.shape
    shard, items = scales.shape
    nsel = cluster_ids.shape[1]
    nblk, ntow = lax.axis_size("blk"), lax.axis_size("tower")
    slots = shard * nblk
    part = shard // ntow
    cand = nsel * items
    ngroup = lax.axis_size("group")
    mine, blk_me, tow_me = lax.axis_index("group"), lax.axis_index("blk"), lax.axis_index("tower")
    group_peers, blk_peers, tow_peers = peers("group"), peers("blk"), peers("tower")
    per = nq // ngroup
    split = (items // ntow) % 8 == 0
    vmem = pl.BlockSpec(memory_space=pltpu.VMEM)
    hbm = pl.BlockSpec(memory_space=pltpu.HBM)
    pin = functools.partial(pltpu.with_memory_space_constraint, memory_space=pltpu.HBM)
    params = pltpu.CompilerParams(vmem_limit_bytes=VMEM_LIMIT)
    flat_panels = panels.reshape(shard * items, width)
    flat_scales = scales.T

    message = pl.pallas_call(
        functools.partial(panel_message_kernel, part * items),
        out_shape=jax.ShapeDtypeStruct((part * items + items, width), panels.dtype),
        in_specs=[hbm, hbm],
        out_specs=vmem,
        scratch_shapes=[
            pltpu.VMEM((items, shard), scales.dtype),
            pltpu.SemaphoreType.DMA((2,)),
        ],
        compiler_params=params,
        name="panel_message",
    )(pin(flat_panels), pin(flat_scales))
    pieces = []
    for to, source, pattern in blk_peers:
        piece = lax.ppermute(message, "blk", pattern)
        pieces.append(piece)
        for _, tow_source, tow_pattern in tow_peers:
            pieces.append(lax.ppermute(piece, "tower", tow_pattern))

    def targets():
        return [to for to, _, _ in peers("group")]

    leaving = pl.pallas_call(
        functools.partial(query_message_kernel, per, items, targets),
        out_shape=[jax.ShapeDtypeStruct((rows + TILE, width), queries.dtype)] * (nq - per),
        in_specs=[hbm, hbm, hbm],
        out_specs=[vmem] * (nq - per),
        scratch_shapes=[
            pltpu.VMEM(cluster_ids.shape, jnp.int32),
            pltpu.VMEM(positives.shape, jnp.int32),
            pltpu.VMEM((TILE, width), jnp.float32),
            pltpu.SemaphoreType.DMA((nq - per + 2,)),
        ],
        compiler_params=params,
        name="query_message",
    )(pin(queries), pin(cluster_ids), pin(positives))
    arrived = [
        lax.ppermute(leaving[n * per + i], "group", pattern)
        for n, (_, _, pattern) in enumerate(group_peers)
        for i in range(per)
    ]
    dims = (nq, per, ntow, len(pieces), rows, nsel, items, slots, shard, split)
    sent_rows = slots * items // ntow
    keep_rows = sent_rows if split else slots * items
    n_send = ntow - 1 if split else 0
    grad_shape = (slots, ntow, items // ntow, width) if split else (slots * items, width)
    results = pl.pallas_call(
        functools.partial(score_kernel, dims),
        out_shape=[pltpu.VMEM((rows + TILE, width), jnp.bfloat16)] * nq
        + [pltpu.VMEM((keep_rows, width), jnp.float32)]
        + [pltpu.VMEM((sent_rows, width), jnp.bfloat16)] * n_send,
        in_specs=[hbm] * 6 + [vmem] * (nq - per + len(pieces)),
        out_specs=[vmem] * (nq + 1 + n_send),
        scratch_shapes=[
            pltpu.VMEM((slots * items, width), jnp.bfloat16),
            pltpu.VMEM((slots * items, LANES), jnp.float32),
            pltpu.VMEM((per, rows, width), jnp.bfloat16),
            pltpu.VMEM((2, cand, rows), jnp.float32),
            pltpu.VMEM((2, cand, width), jnp.bfloat16),
            pltpu.VMEM((2, cand, LANES), jnp.float32),
            pltpu.VMEM((2, cand, rows), jnp.bfloat16),
            pltpu.VMEM((2, cand, width), jnp.float32),
            pltpu.VMEM(grad_shape, jnp.float32),
            pltpu.VMEM((nq, 8, rows), jnp.int32),
            pltpu.SMEM(owner_map.shape, jnp.int32),
            pltpu.SMEM(cluster_ids.shape, jnp.int32),
            pltpu.SMEM((nq, 8, LANES), jnp.int32),
            pltpu.VMEM((nq, 8, LANES), jnp.int32),
            pltpu.VMEM(positives.shape, jnp.int32),
            pltpu.VMEM(flat_scales.shape, flat_scales.dtype),
            pltpu.SemaphoreType.DMA((5 + nq,)),
        ],
        compiler_params=params,
        name="score",
    )(
        pin(owner_map),
        pin(cluster_ids),
        pin(positives),
        pin(flat_scales),
        pin(queries),
        pin(flat_panels),
        *arrived,
        *pieces,
    )
    query_grads, keep, sends = results[:nq], results[nq], results[nq + 1 :]

    def partners(axis):
        return lax.axis_index(axis), [to for to, _, _ in peers(axis)]

    shard_rows = shard * items // ntow
    if split:
        got = [lax.ppermute(sent, "tower", p) for sent, (_, _, p) in zip(sends, tow_peers)]
        own, *leaving = pl.pallas_call(
            functools.partial(tower_sum_kernel, nblk, functools.partial(partners, "blk")),
            out_shape=[pltpu.VMEM((shard_rows, width), jnp.float32)]
            + [pltpu.VMEM((shard_rows, width), jnp.bfloat16)] * (nblk - 1),
            in_specs=[vmem] * (1 + len(got)),
            out_specs=[vmem] * nblk,
            compiler_params=params,
            name="tower_sum",
        )(keep, *got)
    else:
        by_part = keep.reshape(slots, ntow, items // ntow, width)
        total = lax.dynamic_index_in_dim(by_part, tow_me, 1, keepdims=False)
        for to, _, pattern in tow_peers:
            sent = lax.dynamic_index_in_dim(by_part, to, 1, keepdims=False)
            sent = sent.astype(jnp.bfloat16)
            total = total + lax.ppermute(sent, "tower", pattern).astype(jnp.float32)
        total = total.reshape(nblk, shard_rows, width)
        own = pick(total, blk_me)
        leaving = [pick(total, to).astype(jnp.bfloat16) for to, _, _ in blk_peers]
    own, *rest = (own, *leaving, *query_grads)
    leaving, query_grads = rest[: nblk - 1], rest[nblk - 1 :]
    terms = [lax.ppermute(sent, "blk", p) for sent, (_, _, p) in zip(leaving, blk_peers)]
    panel_grads = pl.pallas_call(
        shard_sum_kernel,
        out_shape=jax.ShapeDtypeStruct((shard_rows, width), jnp.float32),
        in_specs=[vmem] * nblk,
        out_specs=vmem,
        compiler_params=params,
        cost_estimate=pl.CostEstimate(flops=10**9, bytes_accessed=10**7, transcendentals=0),
        name="shard_sum",
    )(own, *terms).reshape(shard, items // ntow, width)

    blocks = list(query_grads[:per])
    for n, (to, _, pattern) in enumerate(group_peers):
        home = [(d, s) for s, d in pattern]
        for block in query_grads[(n + 1) * per : (n + 2) * per]:
            blocks.append(lax.ppermute(block, "group", home))
    back_q, back_l = pl.pallas_call(
        functools.partial(home_kernel, per, functools.partial(partners, "group")),
        out_shape=[
            pltpu.HBM((nq, rows, width), jnp.bfloat16),
            jax.ShapeDtypeStruct((nq, rows), jnp.bfloat16),
        ],
        in_specs=[vmem] * nq,
        out_specs=[hbm, vmem],
        scratch_shapes=[pltpu.SemaphoreType.DMA((nq,))],
        compiler_params=params,
        name="home",
    )(*blocks)
    return back_l, back_q, panel_grads


def solution(mesh):
    return jax.shard_map(
        shards,
        mesh=mesh,
        in_specs=(
            P(("tower", "group", "blk"), None, None),
            P(("tower", "group", "blk"), None),
            P(("tower", "group", "blk"), None),
            P("group", None),
            P(("group", "blk"), None, None),
            P(("group", "blk"), None),
        ),
        out_specs=(
            P(("tower", "group", "blk"), None),
            P(("tower", "group", "blk"), None, None),
            P(("group", "blk"), "tower", None),
        ),
        check_vma=False,
    )
```

```python
import functools
import math

import jax
import jax.numpy as jnp
from jax import lax
from jax.experimental import pallas as pl
from jax.experimental.pallas import tpu as pltpu
from jax.sharding import PartitionSpec as P

VMEM_LIMIT = 40 * 1024 * 1024
LANES = 128
TILE = 16
ORDER = (
    (("g", 0), ("s", 0), ("p", 0)),
    (("g", 1), ("s", 1), ("e", 0), ("w", 0), ("t", 0), ("p", 1), ("q", 0), ("a", 0)),
    (),
)
LN2 = math.log(2.0)
COST = 10**10


def peers(axis):
    n = lax.axis_size(axis)
    me = lax.axis_index(axis)
    if n & (n - 1) == 0:
        return [(me ^ k, me ^ k, [(i, i ^ k) for i in range(n)]) for k in range(1, n)]
    return [
        (lax.rem(me + k, n), lax.rem(me + n - k, n), [(i, (i + k) % n) for i in range(n)])
        for k in range(1, n)
    ]


def pick(array, index):
    return lax.dynamic_index_in_dim(array, index, 0, keepdims=False)


def message_kernel(per, part_rows, targets, panels, scales, queries, ids_far, pos_far, *refs):
    (message, *outs, held, ids, positives, marks, sems) = refs
    rows, nsel = queries.shape[1], ids_far.shape[1]
    items, shard = scales.shape
    reps = rows // LANES
    copies = []

    def fetch(source, target):
        copies.append(pltpu.make_async_copy(source, target, sems.at[len(copies)]))
        copies[-1].start()

    start = pl.multiple_of(lax.axis_index("tower") * part_rows, TILE)
    fetch(ids_far, ids)
    fetch(pos_far, positives)
    fetch(scales, held)
    fetch(panels.at[pl.ds(start, part_rows), :], message.at[0:part_rows, :])
    goal = [to * per + i for to in targets() for i in range(per)]
    for block, out in zip(goal, outs):
        fetch(queries.at[block], out.at[0:rows, :])
    for copy in copies[:3]:
        copy.wait()
    below = pl.ds(part_rows, items)
    message[below, :] = jnp.zeros((items, message.shape[1]), message.dtype)
    message[below, 0:shard] = held[...]
    for block, out in zip(goal, outs):
        place = positives[pl.ds(block, 1), :]
        marks[...] = jnp.zeros_like(marks)
        for c in range(reps):
            chunk = place[:, c * LANES : (c + 1) * LANES]
            marks[c : c + 1, 0:LANES] = (chunk // items).astype(jnp.float32)
            marks[c : c + 1, LANES : 2 * LANES] = (chunk % items).astype(jnp.float32)
        marks[reps : reps + 1, 0:nsel] = ids[pl.ds(block, 1), :].astype(jnp.float32)
        out[rows : rows + TILE, :] = marks[...].astype(out.dtype)
    for copy in copies[3:]:
        copy.wait()


def list_kernel(items, count, *refs):
    messages, places, lists = refs[:count], refs[-2 * count : -count], refs[-count:]
    for message, place, ids in zip(messages, places, lists):
        rows = message.shape[0] - TILE
        reps = rows // LANES
        marks = message[rows : rows + TILE, :].astype(jnp.float32)
        found = [
            marks[n : n + 1, 0:LANES] * items + marks[n : n + 1, LANES : 2 * LANES]
            for n in range(reps)
        ]
        found = jnp.concatenate(found, axis=1).astype(jnp.int32)
        place[...] = jnp.broadcast_to(found, place.shape)
        ids[...] = jnp.broadcast_to(marks[reps : reps + 1, 0:LANES], ids.shape).astype(jnp.int32)


def score_kernel(dims, *refs):
    nq, nlocal, ntow, n_piece, rows, nsel, items, slots, shard, split = dims
    refs = list(refs)

    def take(n):
        out, refs[:] = refs[:n], refs[n:]
        return out

    owner_far, ids_far, pos_far, scale_far, queries, own = take(6)
    messages = take(nq - nlocal)
    places = take(nq - nlocal)
    lists = take(nq - nlocal)
    pieces = take(n_piece)
    outs = take(nq)
    (keep,) = take(1)
    sends = take(ntow - 1 if split else 0)
    (panel, wide, query, score, sel, sel_wide, weight, term, grad, place) = refs[:10]
    (owner, ids, far_ids, pos_own, scale_own, sems) = refs[10:]
    part = shard // ntow
    cand = nsel * items
    width = panel.shape[1]
    mine, blk_me, tow_me = lax.axis_index("group"), lax.axis_index("blk"), lax.axis_index("tower")
    blk_to = [to for _, to, _ in peers("blk")]
    tow_to = [to for _, to, _ in peers("tower")]
    copies = []

    def fetch(source, target):
        copies.append(pltpu.make_async_copy(source, target, sems.at[len(copies)]))
        copies[-1].start()
        return copies[-1]

    def rows_at(slot, count):
        return pl.ds(pl.multiple_of(slot * items, TILE), count * items)

    early = [fetch(ids_far, ids), fetch(owner_far, owner)]
    early.append(fetch(scale_far, scale_own))
    early.append(fetch(pos_far, pos_own))
    early.append(fetch(own, panel.at[rows_at(blk_me * shard, shard), :]))
    local = [fetch(queries.at[mine * nlocal + n], query.at[n]) for n in range(nlocal)]
    for n, piece in enumerate(pieces):
        first = blk_to[n // ntow] * shard + ([tow_me] + tow_to)[n % ntow] * part
        panel[rows_at(first, part), :] = piece[0 : part * items, :]
    grad[...] = jnp.zeros_like(grad)

    def block_rows(b):
        return query[b] if b < nlocal else messages[b - nlocal][0:rows, :]

    reps = rows // LANES
    moved = []

    for b in range(nlocal, nq):
        place[b] = places[b - nlocal][...]
        moved.append(fetch(lists[b - nlocal], far_ids.at[b]))
    early[2].wait()
    item_of = lax.broadcasted_iota(jnp.int32, (shard * items, items), 0) % items
    spread = item_of == lax.broadcasted_iota(jnp.int32, (shard * items, items), 1)
    spread = spread.astype(jnp.bfloat16)

    def widen(values, at):
        lanes = values.shape[1]
        of_item = jnp.dot(spread, values, preferred_element_type=jnp.float32)
        slot_of = lax.broadcasted_iota(jnp.int32, (shard * items, lanes), 0) // items
        mine = slot_of == lax.broadcasted_iota(jnp.int32, (shard * items, lanes), 1)
        wide[at, :] = jnp.dot(
            jnp.where(mine, of_item, 0.0).astype(jnp.bfloat16),
            jnp.ones((lanes, LANES), jnp.bfloat16),
            preferred_element_type=jnp.float32,
        ) * (1.0 / LN2)

    widen(scale_own[...], rows_at(blk_me * shard, shard))
    for n, to in enumerate(blk_to):
        widen(pieces[n * ntow][part * items : part * items + items, 0:LANES], rows_at(to * shard, shard))

    line = lax.broadcasted_iota(jnp.int32, (8, LANES), 0)
    state = [{} for _ in range(nq)]
    for n, copy in enumerate(early + local + moved):
        if n != 2:
            copy.wait()
    for b in range(nlocal):
        place[b] = jnp.broadcast_to(pos_own[pl.ds(mine * nlocal + b, 1), :], (8, rows))

    def slot_of(b, j):
        if b < nlocal:
            return owner[0, ids[mine * nlocal + b, j]]
        return owner[0, far_ids[b, 0, j]]

    def gather(b):
        two = b % 2
        for j in range(nsel):
            at = slice(j * items, (j + 1) * items)
            slot = rows_at(slot_of(b, j), 1)
            sel[two, at, :] = panel[slot, :]
            sel_wide[two, at, :] = wide[slot, :]

    def scores(b):
        score[b % 2] = lax.dot_general(
            sel[b % 2],
            block_rows(b),
            (((1,), (1,)), ((), ())),
            preferred_element_type=jnp.float32,
        )

    def spread_scale(two, first):
        return jnp.tile(sel_wide[two, first : first + 8, :], (1, reps))

    def is_positive(pos, first):
        return jnp.tile(line + first, (1, reps)) == pos

    def peaks(b):
        two = b % 2
        peak = jnp.full((8, rows), -jnp.inf, jnp.float32)
        for first in range(0, cand, 8):
            s = score[two, first : first + 8, :] * spread_scale(two, first)
            score[two, first : first + 8, :] = s
            peak = jnp.maximum(peak, s)
        state[b]["top"] = jnp.max(peak, axis=0, keepdims=True)

    def exps(b):
        two, top, pos = b % 2, state[b]["top"], place[b]
        total = jnp.zeros((8, rows), jnp.float32)
        pick = jnp.zeros((8, rows), jnp.float32)
        for first in range(0, cand, 8):
            s = score[two, first : first + 8, :]
            e = jnp.exp2(s - top)
            score[two, first : first + 8, :] = e
            total = total + e
            pick = jnp.where(is_positive(pos, first), s, pick)
        total = jnp.sum(total, axis=0, keepdims=True)
        picked = jnp.sum(pick, axis=0, keepdims=True)
        loss = (top - picked) * LN2 + jnp.log(total)
        state[b]["inverse"] = LN2 / total
        row_of = lax.broadcasted_iota(jnp.int32, (TILE, LANES), 0)
        below = jnp.zeros((TILE, LANES), jnp.float32)
        for n in range(reps):
            below = jnp.where(row_of == n, loss[:, n * LANES : (n + 1) * LANES], below)
        outs[b][rows : rows + TILE, :] = jnp.zeros((TILE, width), jnp.bfloat16)
        outs[b][rows : rows + TILE, 0:LANES] = below.astype(jnp.bfloat16)

    def weigh(b):
        two, inverse, pos = b % 2, state[b]["inverse"], place[b]
        for start in range(0, cand, TILE):
            halves = []
            for first in range(start, start + TILE, 8):
                chance = score[two, first : first + 8, :] * inverse
                chance = jnp.where(is_positive(pos, first), chance - LN2, chance)
                halves.append(chance * spread_scale(two, first))
            weight[two, start : start + TILE, :] = jnp.concatenate(halves, axis=0).astype(
                jnp.bfloat16
            )

    def panel_terms(b):
        term[b % 2] = jnp.dot(
            weight[b % 2], block_rows(b), preferred_element_type=jnp.float32
        )

    def scatter(b):
        for j in range(nsel):
            slot = slot_of(b, j)
            add = term[b % 2, j * items : (j + 1) * items, :]
            if split:
                grad[slot] += add.reshape(ntow, items // ntow, width)
            else:
                grad[rows_at(slot, 1), :] += add

    def query_terms(b):
        outs[b][0:rows, :] = lax.dot_general(
            weight[b % 2],
            sel[b % 2],
            (((0,), (0,)), ((), ())),
            preferred_element_type=jnp.float32,
        ).astype(jnp.bfloat16)

    jobs = dict(g=gather, s=scores, p=peaks, e=exps, w=weigh, t=panel_terms, a=scatter, q=query_terms)
    for name, shift in ORDER[0]:
        if shift < nq:
            jobs[name](shift)
    for b in range(nq):
        for name, shift in ORDER[1]:
            if 0 <= b + shift < nq:
                jobs[name](b + shift)
    for name, shift in ORDER[2]:
        jobs[name](nq - 1 + shift)
    if split:
        keep[...] = grad[:, tow_me].reshape(keep.shape)
        for to, send in zip([to for to, _, _ in peers("tower")], sends):
            send[...] = grad[:, to].reshape(send.shape).astype(send.dtype)
    else:
        keep[...] = grad[...]


def tower_sum_kernel(nblk, partners, keep, *refs):
    got, outs = refs[: len(refs) - nblk], refs[len(refs) - nblk :]
    me, to = partners()
    rows = keep.shape[0] // nblk
    for owner, out in zip([me] + to, outs):
        at = pl.ds(pl.multiple_of(owner * rows, TILE), rows)
        total = keep[at, :]
        for term in got:
            total = total + term[at, :].astype(jnp.float32)
        out[...] = total.astype(out.dtype)


def shard_sum_kernel(own, *refs):
    total = own[...]
    for term in refs[:-1]:
        total = total + term[...].astype(jnp.float32)
    refs[-1][...] = total


def home_kernel(per, partners, *refs):
    (*blocks, grads, losses, sems) = refs
    nq, rows, _ = grads.shape
    me, to = partners()
    copies = []
    lines = lax.broadcasted_iota(jnp.int32, (nq, LANES), 0)
    parts = [jnp.zeros((nq, LANES), jnp.float32)] * (rows // LANES)
    for n, block in enumerate(blocks):
        place = ([me] + to)[n // per] * per + n % per
        copies.append(
            pltpu.make_async_copy(block.at[0:rows, :], grads.at[place], sems.at[n])
        )
        copies[-1].start()
    for n, block in enumerate(blocks):
        place = ([me] + to)[n // per] * per + n % per
        tile = block[rows : rows + TILE, 0:LANES].astype(jnp.float32)
        parts = [jnp.where(lines == place, tile[c : c + 1, :], p) for c, p in enumerate(parts)]
    losses[...] = jnp.concatenate(parts, axis=1).astype(losses.dtype)
    for copy in copies:
        copy.wait()


def shards(queries, cluster_ids, positives, owner_map, panels, scales):
    nq, rows, width = queries.shape
    shard, items = scales.shape
    nsel = cluster_ids.shape[1]
    nblk, ntow = lax.axis_size("blk"), lax.axis_size("tower")
    slots = shard * nblk
    part = shard // ntow
    cand = nsel * items
    ngroup = lax.axis_size("group")
    mine, blk_me, tow_me = lax.axis_index("group"), lax.axis_index("blk"), lax.axis_index("tower")
    group_peers, blk_peers, tow_peers = peers("group"), peers("blk"), peers("tower")
    per = nq // ngroup
    split = (items // ntow) % 8 == 0
    vmem = pl.BlockSpec(memory_space=pltpu.VMEM)
    hbm = pl.BlockSpec(memory_space=pltpu.HBM)
    pin = functools.partial(pltpu.with_memory_space_constraint, memory_space=pltpu.HBM)
    params = pltpu.CompilerParams(vmem_limit_bytes=VMEM_LIMIT)
    flat_panels = panels.reshape(shard * items, width)
    flat_scales = scales.T

    def targets():
        return [to for to, _, _ in peers("group")]

    message, *leaving = pl.pallas_call(
        functools.partial(message_kernel, per, part * items, targets),
        out_shape=[jax.ShapeDtypeStruct((part * items + items, width), panels.dtype)]
        + [jax.ShapeDtypeStruct((rows + TILE, width), queries.dtype)] * (nq - per),
        in_specs=[hbm] * 5,
        out_specs=[vmem] * (1 + nq - per),
        scratch_shapes=[
            pltpu.VMEM(flat_scales.shape, scales.dtype),
            pltpu.VMEM(cluster_ids.shape, jnp.int32),
            pltpu.VMEM(positives.shape, jnp.int32),
            pltpu.VMEM((TILE, width), jnp.float32),
            pltpu.SemaphoreType.DMA((4 + nq - per,)),
        ],
        compiler_params=params,
        name="messages",
    )(pin(flat_panels), pin(flat_scales), pin(queries), pin(cluster_ids), pin(positives))

    pieces = []
    near = [lax.ppermute(message, "blk", pattern) for _, _, pattern in blk_peers[:2]]
    for n, (_, _, pattern) in enumerate(blk_peers):
        if n < 2:
            piece = near[n]
        elif nblk == 4:
            piece = lax.ppermute(near[1], "blk", blk_peers[0][2])
        else:
            piece = lax.ppermute(message, "blk", pattern)
        pieces.append(piece)
        for _, tow_source, tow_pattern in tow_peers:
            pieces.append(lax.ppermute(piece, "tower", tow_pattern))

    arrived = [
        lax.ppermute(leaving[n * per + i], "group", pattern)
        for n, (_, _, pattern) in enumerate(group_peers)
        for i in range(per)
    ]
    far, first = nq - per, pieces[1:2]
    lists = pl.pallas_call(
        functools.partial(list_kernel, items, far),
        out_shape=[jax.ShapeDtypeStruct((8, rows), jnp.int32)] * far
        + [jax.ShapeDtypeStruct((8, LANES), jnp.int32)] * far,
        in_specs=[vmem] * (far + len(first)),
        out_specs=[vmem] * (2 * far),
        compiler_params=params,
        cost_estimate=pl.CostEstimate(flops=COST, bytes_accessed=COST // 1000, transcendentals=0),
        name="lists",
    )(*arrived, *first)
    dims = (nq, per, ntow, len(pieces), rows, nsel, items, slots, shard, split)
    sent_rows = slots * items // ntow
    keep_rows = sent_rows if split else slots * items
    n_send = ntow - 1 if split else 0
    grad_shape = (slots, ntow, items // ntow, width) if split else (slots * items, width)
    results = pl.pallas_call(
        functools.partial(score_kernel, dims),
        out_shape=[pltpu.VMEM((rows + TILE, width), jnp.bfloat16)] * nq
        + [pltpu.VMEM((keep_rows, width), jnp.float32)]
        + [pltpu.VMEM((sent_rows, width), jnp.bfloat16)] * n_send,
        in_specs=[hbm] * 6 + [vmem] * (3 * (nq - per) + len(pieces)),
        out_specs=[vmem] * (nq + 1 + n_send),
        scratch_shapes=[
            pltpu.VMEM((slots * items, width), jnp.bfloat16),
            pltpu.VMEM((slots * items, LANES), jnp.float32),
            pltpu.VMEM((per, rows, width), jnp.bfloat16),
            pltpu.VMEM((2, cand, rows), jnp.float32),
            pltpu.VMEM((2, cand, width), jnp.bfloat16),
            pltpu.VMEM((2, cand, LANES), jnp.float32),
            pltpu.VMEM((2, cand, rows), jnp.bfloat16),
            pltpu.VMEM((2, cand, width), jnp.float32),
            pltpu.VMEM(grad_shape, jnp.float32),
            pltpu.VMEM((nq, 8, rows), jnp.int32),
            pltpu.SMEM(owner_map.shape, jnp.int32),
            pltpu.SMEM(cluster_ids.shape, jnp.int32),
            pltpu.SMEM((nq, 8, LANES), jnp.int32),
            pltpu.VMEM(positives.shape, jnp.int32),
            pltpu.VMEM(flat_scales.shape, flat_scales.dtype),
            pltpu.SemaphoreType.DMA((5 + nq,)),
        ],
        compiler_params=params,
        name="score",
    )(
        pin(owner_map),
        pin(cluster_ids),
        pin(positives),
        pin(flat_scales),
        pin(queries),
        pin(flat_panels),
        *arrived,
        *lists,
        *pieces,
    )
    query_grads, keep, sends = results[:nq], results[nq], results[nq + 1 :]

    def partners(axis):
        return lax.axis_index(axis), [to for to, _, _ in peers(axis)]

    shard_rows = shard * items // ntow
    if split:
        got = [lax.ppermute(sent, "tower", p) for sent, (_, _, p) in zip(sends, tow_peers)]
        own, *leaving = pl.pallas_call(
            functools.partial(tower_sum_kernel, nblk, functools.partial(partners, "blk")),
            out_shape=[pltpu.VMEM((shard_rows, width), jnp.float32)]
            + [pltpu.VMEM((shard_rows, width), jnp.bfloat16)] * (nblk - 1),
            in_specs=[vmem] * (1 + len(got)),
            out_specs=[vmem] * nblk,
            compiler_params=params,
            name="tower_sum",
        )(keep, *got)
    else:
        by_part = keep.reshape(slots, ntow, items // ntow, width)
        total = lax.dynamic_index_in_dim(by_part, tow_me, 1, keepdims=False)
        for to, _, pattern in tow_peers:
            sent = lax.dynamic_index_in_dim(by_part, to, 1, keepdims=False)
            sent = sent.astype(jnp.bfloat16)
            total = total + lax.ppermute(sent, "tower", pattern).astype(jnp.float32)
        total = total.reshape(nblk, shard_rows, width)
        own = pick(total, blk_me)
        leaving = [pick(total, to).astype(jnp.bfloat16) for to, _, _ in blk_peers]
    own, *rest = (own, *leaving, *query_grads)
    leaving, query_grads = rest[: nblk - 1], rest[nblk - 1 :]
    terms = [lax.ppermute(sent, "blk", p) for sent, (_, _, p) in zip(leaving, blk_peers)]
    panel_grads = pl.pallas_call(
        shard_sum_kernel,
        out_shape=jax.ShapeDtypeStruct((shard_rows, width), jnp.float32),
        in_specs=[vmem] * nblk,
        out_specs=vmem,
        compiler_params=params,
        cost_estimate=pl.CostEstimate(flops=10**9, bytes_accessed=10**7, transcendentals=0),
        name="shard_sum",
    )(own, *terms).reshape(shard, items // ntow, width)

    blocks = list(query_grads[:per])
    for n, (to, _, pattern) in enumerate(group_peers):
        home = [(d, s) for s, d in pattern]
        for block in query_grads[(n + 1) * per : (n + 2) * per]:
            blocks.append(lax.ppermute(block, "group", home))
    back_q, back_l = pl.pallas_call(
        functools.partial(home_kernel, per, functools.partial(partners, "group")),
        out_shape=[
            pltpu.HBM((nq, rows, width), jnp.bfloat16),
            jax.ShapeDtypeStruct((nq, rows), jnp.bfloat16),
        ],
        in_specs=[vmem] * nq,
        out_specs=[hbm, vmem],
        scratch_shapes=[pltpu.SemaphoreType.DMA((nq,))],
        compiler_params=params,
        name="home",
    )(*blocks)
    return back_l, back_q, panel_grads


def solution(mesh):
    return jax.shard_map(
        shards,
        mesh=mesh,
        in_specs=(
            P(("tower", "group", "blk"), None, None),
            P(("tower", "group", "blk"), None),
            P(("tower", "group", "blk"), None),
            P("group", None),
            P(("group", "blk"), None, None),
            P(("group", "blk"), None),
        ),
        out_specs=(
            P(("tower", "group", "blk"), None),
            P(("tower", "group", "blk"), None, None),
            P(("group", "blk"), "tower", None),
        ),
        check_vma=False,
    )
```

```python
import functools
import math

import jax
import jax.numpy as jnp
from jax import lax
from jax.experimental import pallas as pl
from jax.experimental.pallas import tpu as pltpu
from jax.sharding import PartitionSpec as P

VMEM_LIMIT = 40 * 1024 * 1024
LANES = 128
TILE = 16
ORDER = (
    (("g", 0), ("s", 0), ("p", 0)),
    (("g", 1), ("s", 1), ("e", 0), ("w", 0), ("t", 0), ("p", 1), ("q", 0), ("a", 0)),
    (),
)
LN2 = math.log(2.0)
COST = 10**10


def peers(axis):
    n = lax.axis_size(axis)
    me = lax.axis_index(axis)
    if n & (n - 1) == 0:
        return [(me ^ k, me ^ k, [(i, i ^ k) for i in range(n)]) for k in range(1, n)]
    return [
        (lax.rem(me + k, n), lax.rem(me + n - k, n), [(i, (i + k) % n) for i in range(n)])
        for k in range(1, n)
    ]


def pick(array, index):
    return lax.dynamic_index_in_dim(array, index, 0, keepdims=False)


def message_kernel(per, part_rows, targets, panels, scales, queries, ids_far, pos_far, *refs):
    (message, *outs, held, ids, positives, marks, sems) = refs
    rows, nsel = queries.shape[1], ids_far.shape[1]
    items, shard = scales.shape
    reps = rows // LANES
    copies = []

    def fetch(source, target):
        copies.append(pltpu.make_async_copy(source, target, sems.at[len(copies)]))
        copies[-1].start()

    start = pl.multiple_of(lax.axis_index("tower") * part_rows, TILE)
    fetch(ids_far, ids)
    fetch(pos_far, positives)
    fetch(scales, held)
    fetch(panels.at[pl.ds(start, part_rows), :], message.at[0:part_rows, :])
    goal = [to * per + i for to in targets() for i in range(per)]
    for block, out in zip(goal, outs):
        fetch(queries.at[block], out.at[0:rows, :])
    for copy in copies[:3]:
        copy.wait()
    below = pl.ds(part_rows, items)
    message[below, :] = jnp.zeros((items, message.shape[1]), message.dtype)
    message[below, 0:shard] = held[...]
    for block, out in zip(goal, outs):
        place = positives[pl.ds(block, 1), :]
        marks[...] = jnp.zeros_like(marks)
        for c in range(reps):
            chunk = place[:, c * LANES : (c + 1) * LANES]
            marks[c : c + 1, 0:LANES] = (chunk // items).astype(jnp.float32)
            marks[c : c + 1, LANES : 2 * LANES] = (chunk % items).astype(jnp.float32)
        marks[reps : reps + 1, 0:nsel] = ids[pl.ds(block, 1), :].astype(jnp.float32)
        out[rows : rows + TILE, :] = marks[...].astype(out.dtype)
    for copy in copies[3:]:
        copy.wait()


def list_kernel(items, count, *refs):
    messages, places, lists = refs[:count], refs[-2 * count : -count], refs[-count:]
    for message, place, ids in zip(messages, places, lists):
        rows = message.shape[0] - TILE
        reps = rows // LANES
        marks = message[rows : rows + TILE, :].astype(jnp.float32)
        found = [
            marks[n : n + 1, 0:LANES] * items + marks[n : n + 1, LANES : 2 * LANES]
            for n in range(reps)
        ]
        found = jnp.concatenate(found, axis=1).astype(jnp.int32)
        place[...] = jnp.broadcast_to(found, place.shape)
        ids[...] = jnp.broadcast_to(marks[reps : reps + 1, 0:LANES], ids.shape).astype(jnp.int32)


def score_kernel(dims, *refs):
    nq, nlocal, ntow, n_piece, rows, nsel, items, slots, shard, split = dims
    refs = list(refs)

    def take(n):
        out, refs[:] = refs[:n], refs[n:]
        return out

    owner_far, ids_far, pos_far, scale_far, queries, own = take(6)
    messages = take(nq - nlocal)
    places = take(nq - nlocal)
    lists = take(nq - nlocal)
    pieces = take(n_piece)
    outs = take(nq)
    (keep,) = take(1)
    sends = take(ntow - 1 if split else 0)
    (panel, wide, query, score, sel, sel_wide, weight, term, grad, place) = refs[:10]
    (owner, ids, far_ids, pos_own, scale_own, sems) = refs[10:]
    part = shard // ntow
    cand = nsel * items
    width = panel.shape[1]
    mine, blk_me, tow_me = lax.axis_index("group"), lax.axis_index("blk"), lax.axis_index("tower")
    blk_to = [to for _, to, _ in peers("blk")]
    tow_to = [to for _, to, _ in peers("tower")]
    copies = []

    def fetch(source, target):
        copies.append(pltpu.make_async_copy(source, target, sems.at[len(copies)]))
        copies[-1].start()
        return copies[-1]

    def rows_at(slot, count):
        return pl.ds(pl.multiple_of(slot * items, TILE), count * items)

    early = [fetch(ids_far, ids), fetch(owner_far, owner)]
    early.append(fetch(scale_far, scale_own))
    early.append(fetch(pos_far, pos_own))
    early.append(fetch(own, panel.at[rows_at(blk_me * shard, shard), :]))
    local = [fetch(queries.at[mine * nlocal + n], query.at[n]) for n in range(nlocal)]
    for n, piece in enumerate(pieces):
        first = blk_to[n // ntow] * shard + ([tow_me] + tow_to)[n % ntow] * part
        panel[rows_at(first, part), :] = piece[0 : part * items, :]
    grad[...] = jnp.zeros_like(grad)

    def block_rows(b):
        return query[b] if b < nlocal else messages[b - nlocal][0:rows, :]

    reps = rows // LANES
    moved = []

    for b in range(nlocal, nq):
        place[b] = places[b - nlocal][...]
        moved.append(fetch(lists[b - nlocal], far_ids.at[b]))
    early[2].wait()
    item_of = lax.broadcasted_iota(jnp.int32, (shard * items, items), 0) % items
    spread = item_of == lax.broadcasted_iota(jnp.int32, (shard * items, items), 1)
    spread = spread.astype(jnp.bfloat16)

    def widen(values, at):
        lanes = values.shape[1]
        of_item = jnp.dot(spread, values, preferred_element_type=jnp.float32)
        slot_of = lax.broadcasted_iota(jnp.int32, (shard * items, lanes), 0) // items
        mine = slot_of == lax.broadcasted_iota(jnp.int32, (shard * items, lanes), 1)
        wide[at, :] = jnp.dot(
            jnp.where(mine, of_item, 0.0).astype(jnp.bfloat16),
            jnp.ones((lanes, LANES), jnp.bfloat16),
            preferred_element_type=jnp.float32,
        ) * (1.0 / LN2)

    widen(scale_own[...], rows_at(blk_me * shard, shard))
    for n, to in enumerate(blk_to):
        widen(pieces[n * ntow][part * items : part * items + items, 0:LANES], rows_at(to * shard, shard))

    line = lax.broadcasted_iota(jnp.int32, (8, LANES), 0)
    state = [{} for _ in range(nq)]
    for n, copy in enumerate(early + local + moved):
        if n != 2:
            copy.wait()
    for b in range(nlocal):
        place[b] = jnp.broadcast_to(pos_own[pl.ds(mine * nlocal + b, 1), :], (8, rows))

    def slot_of(b, j):
        if b < nlocal:
            return owner[0, ids[mine * nlocal + b, j]]
        return owner[0, far_ids[b, 0, j]]

    def gather(b):
        two = b % 2
        for j in range(nsel):
            at = slice(j * items, (j + 1) * items)
            slot = rows_at(slot_of(b, j), 1)
            sel[two, at, :] = panel[slot, :]
            sel_wide[two, at, :] = wide[slot, :]

    def scores(b):
        score[b % 2] = lax.dot_general(
            sel[b % 2],
            block_rows(b),
            (((1,), (1,)), ((), ())),
            preferred_element_type=jnp.float32,
        )

    def spread_scale(two, first):
        return jnp.tile(sel_wide[two, first : first + 8, :], (1, reps))

    def is_positive(pos, first):
        return jnp.tile(line + first, (1, reps)) == pos

    def peaks(b):
        two = b % 2
        peak = jnp.full((8, rows), -jnp.inf, jnp.float32)
        for first in range(0, cand, 8):
            s = score[two, first : first + 8, :] * spread_scale(two, first)
            score[two, first : first + 8, :] = s
            peak = jnp.maximum(peak, s)
        state[b]["top"] = jnp.max(peak, axis=0, keepdims=True)

    def exps(b):
        two, top, pos = b % 2, state[b]["top"], place[b]
        total = jnp.zeros((8, rows), jnp.float32)
        pick = jnp.zeros((8, rows), jnp.float32)
        for first in range(0, cand, 8):
            s = score[two, first : first + 8, :]
            e = jnp.exp2(s - top)
            score[two, first : first + 8, :] = e
            total = total + e
            pick = jnp.where(is_positive(pos, first), s, pick)
        total = jnp.sum(total, axis=0, keepdims=True)
        picked = jnp.sum(pick, axis=0, keepdims=True)
        loss = (top - picked) * LN2 + jnp.log(total)
        state[b]["inverse"] = LN2 / total
        row_of = lax.broadcasted_iota(jnp.int32, (TILE, LANES), 0)
        below = jnp.zeros((TILE, LANES), jnp.float32)
        for n in range(reps):
            below = jnp.where(row_of == n, loss[:, n * LANES : (n + 1) * LANES], below)
        outs[b][rows : rows + TILE, :] = jnp.zeros((TILE, width), jnp.bfloat16)
        outs[b][rows : rows + TILE, 0:LANES] = below.astype(jnp.bfloat16)

    def weigh(b):
        two, inverse, pos = b % 2, state[b]["inverse"], place[b]
        for start in range(0, cand, TILE):
            halves = []
            for first in range(start, start + TILE, 8):
                chance = score[two, first : first + 8, :] * inverse
                chance = jnp.where(is_positive(pos, first), chance - LN2, chance)
                halves.append(chance * spread_scale(two, first))
            weight[two, start : start + TILE, :] = jnp.concatenate(halves, axis=0).astype(
                jnp.bfloat16
            )

    def panel_terms(b):
        term[b % 2] = jnp.dot(
            weight[b % 2], block_rows(b), preferred_element_type=jnp.float32
        )

    def scatter(b):
        for j in range(nsel):
            slot = slot_of(b, j)
            add = term[b % 2, j * items : (j + 1) * items, :]
            if split:
                grad[slot] += add.reshape(ntow, items // ntow, width)
            else:
                grad[rows_at(slot, 1), :] += add

    def query_terms(b):
        outs[b][0:rows, :] = lax.dot_general(
            weight[b % 2],
            sel[b % 2],
            (((0,), (0,)), ((), ())),
            preferred_element_type=jnp.float32,
        ).astype(jnp.bfloat16)

    jobs = dict(g=gather, s=scores, p=peaks, e=exps, w=weigh, t=panel_terms, a=scatter, q=query_terms)
    for name, shift in ORDER[0]:
        if shift < nq:
            jobs[name](shift)
    for b in range(nq):
        for name, shift in ORDER[1]:
            if 0 <= b + shift < nq:
                jobs[name](b + shift)
    for name, shift in ORDER[2]:
        jobs[name](nq - 1 + shift)
    if split:
        keep[...] = grad[:, tow_me].reshape(keep.shape)
        for to, send in zip([to for to, _, _ in peers("tower")], sends):
            send[...] = grad[:, to].reshape(send.shape).astype(send.dtype)
    else:
        keep[...] = grad[...]


def tower_sum_kernel(nblk, partners, keep, *refs):
    got, outs = refs[: len(refs) - nblk], refs[len(refs) - nblk :]
    me, to = partners()
    rows = keep.shape[0] // nblk
    for owner, out in zip([me] + to, outs):
        at = pl.ds(pl.multiple_of(owner * rows, TILE), rows)
        total = keep[at, :]
        for term in got:
            total = total + term[at, :].astype(jnp.float32)
        out[...] = total.astype(out.dtype)


def shard_sum_kernel(*refs):
    (*terms, out) = refs
    total = terms[0][...].astype(jnp.float32)
    for term in terms[1:]:
        total = total + term[...].astype(jnp.float32)
    out[...] = total.astype(out.dtype)


def home_kernel(per, partners, *refs):
    (*blocks, grads, losses, sems) = refs
    nq, rows, _ = grads.shape
    me, to = partners()
    copies = []
    lines = lax.broadcasted_iota(jnp.int32, (nq, LANES), 0)
    parts = [jnp.zeros((nq, LANES), jnp.float32)] * (rows // LANES)
    for n, block in enumerate(blocks):
        place = ([me] + to)[n // per] * per + n % per
        copies.append(
            pltpu.make_async_copy(block.at[0:rows, :], grads.at[place], sems.at[n])
        )
        copies[-1].start()
    for n, block in enumerate(blocks):
        place = ([me] + to)[n // per] * per + n % per
        tile = block[rows : rows + TILE, 0:LANES].astype(jnp.float32)
        parts = [jnp.where(lines == place, tile[c : c + 1, :], p) for c, p in enumerate(parts)]
    losses[...] = jnp.concatenate(parts, axis=1).astype(losses.dtype)
    for copy in copies:
        copy.wait()


def shards(queries, cluster_ids, positives, owner_map, panels, scales):
    nq, rows, width = queries.shape
    shard, items = scales.shape
    nsel = cluster_ids.shape[1]
    nblk, ntow = lax.axis_size("blk"), lax.axis_size("tower")
    slots = shard * nblk
    part = shard // ntow
    cand = nsel * items
    ngroup = lax.axis_size("group")
    mine, blk_me, tow_me = lax.axis_index("group"), lax.axis_index("blk"), lax.axis_index("tower")
    group_peers, blk_peers, tow_peers = peers("group"), peers("blk"), peers("tower")
    per = nq // ngroup
    split = (items // ntow) % 8 == 0
    vmem = pl.BlockSpec(memory_space=pltpu.VMEM)
    hbm = pl.BlockSpec(memory_space=pltpu.HBM)
    pin = functools.partial(pltpu.with_memory_space_constraint, memory_space=pltpu.HBM)
    params = pltpu.CompilerParams(vmem_limit_bytes=VMEM_LIMIT)
    flat_panels = panels.reshape(shard * items, width)
    flat_scales = scales.T

    def targets():
        return [to for to, _, _ in peers("group")]

    message, *leaving = pl.pallas_call(
        functools.partial(message_kernel, per, part * items, targets),
        out_shape=[jax.ShapeDtypeStruct((part * items + items, width), panels.dtype)]
        + [jax.ShapeDtypeStruct((rows + TILE, width), queries.dtype)] * (nq - per),
        in_specs=[hbm] * 5,
        out_specs=[vmem] * (1 + nq - per),
        scratch_shapes=[
            pltpu.VMEM(flat_scales.shape, scales.dtype),
            pltpu.VMEM(cluster_ids.shape, jnp.int32),
            pltpu.VMEM(positives.shape, jnp.int32),
            pltpu.VMEM((TILE, width), jnp.float32),
            pltpu.SemaphoreType.DMA((4 + nq - per,)),
        ],
        compiler_params=params,
        name="messages",
    )(pin(flat_panels), pin(flat_scales), pin(queries), pin(cluster_ids), pin(positives))

    pieces = []
    near = [lax.ppermute(message, "blk", pattern) for _, _, pattern in blk_peers[:2]]
    for n, (_, _, pattern) in enumerate(blk_peers):
        if n < 2:
            piece = near[n]
        elif nblk == 4:
            piece = lax.ppermute(near[1], "blk", blk_peers[0][2])
        else:
            piece = lax.ppermute(message, "blk", pattern)
        pieces.append(piece)
        for _, tow_source, tow_pattern in tow_peers:
            pieces.append(lax.ppermute(piece, "tower", tow_pattern))

    arrived = [
        lax.ppermute(leaving[n * per + i], "group", pattern)
        for n, (_, _, pattern) in enumerate(group_peers)
        for i in range(per)
    ]
    far, first = nq - per, pieces[1:2]
    lists = pl.pallas_call(
        functools.partial(list_kernel, items, far),
        out_shape=[jax.ShapeDtypeStruct((8, rows), jnp.int32)] * far
        + [jax.ShapeDtypeStruct((8, LANES), jnp.int32)] * far,
        in_specs=[vmem] * (far + len(first)),
        out_specs=[vmem] * (2 * far),
        compiler_params=params,
        cost_estimate=pl.CostEstimate(flops=COST, bytes_accessed=COST // 1000, transcendentals=0),
        name="lists",
    )(*arrived, *first)
    dims = (nq, per, ntow, len(pieces), rows, nsel, items, slots, shard, split)
    sent_rows = slots * items // ntow
    keep_rows = sent_rows if split else slots * items
    n_send = ntow - 1 if split else 0
    grad_shape = (slots, ntow, items // ntow, width) if split else (slots * items, width)
    results = pl.pallas_call(
        functools.partial(score_kernel, dims),
        out_shape=[pltpu.VMEM((rows + TILE, width), jnp.bfloat16)] * nq
        + [pltpu.VMEM((keep_rows, width), jnp.float32)]
        + [pltpu.VMEM((sent_rows, width), jnp.bfloat16)] * n_send,
        in_specs=[hbm] * 6 + [vmem] * (3 * (nq - per) + len(pieces)),
        out_specs=[vmem] * (nq + 1 + n_send),
        scratch_shapes=[
            pltpu.VMEM((slots * items, width), jnp.bfloat16),
            pltpu.VMEM((slots * items, LANES), jnp.float32),
            pltpu.VMEM((per, rows, width), jnp.bfloat16),
            pltpu.VMEM((2, cand, rows), jnp.float32),
            pltpu.VMEM((2, cand, width), jnp.bfloat16),
            pltpu.VMEM((2, cand, LANES), jnp.float32),
            pltpu.VMEM((2, cand, rows), jnp.bfloat16),
            pltpu.VMEM((2, cand, width), jnp.float32),
            pltpu.VMEM(grad_shape, jnp.float32),
            pltpu.VMEM((nq, 8, rows), jnp.int32),
            pltpu.SMEM(owner_map.shape, jnp.int32),
            pltpu.SMEM(cluster_ids.shape, jnp.int32),
            pltpu.SMEM((nq, 8, LANES), jnp.int32),
            pltpu.VMEM(positives.shape, jnp.int32),
            pltpu.VMEM(flat_scales.shape, flat_scales.dtype),
            pltpu.SemaphoreType.DMA((5 + nq,)),
        ],
        compiler_params=params,
        name="score",
    )(
        pin(owner_map),
        pin(cluster_ids),
        pin(positives),
        pin(flat_scales),
        pin(queries),
        pin(flat_panels),
        *arrived,
        *lists,
        *pieces,
    )
    query_grads, keep, sends = results[:nq], results[nq], results[nq + 1 :]

    def partners(axis):
        return lax.axis_index(axis), [to for to, _, _ in peers(axis)]

    shard_rows = shard * items // ntow
    wide_terms = [nblk == 4 and n == 1 for n in range(nblk - 1)]
    if split:
        got = [lax.ppermute(sent, "tower", p) for sent, (_, _, p) in zip(sends, tow_peers)]
        own, *leaving = pl.pallas_call(
            functools.partial(tower_sum_kernel, nblk, functools.partial(partners, "blk")),
            out_shape=[pltpu.VMEM((shard_rows, width), jnp.float32)]
            + [
                pltpu.VMEM((shard_rows, width), jnp.float32 if stays else jnp.bfloat16)
                for stays in wide_terms
            ],
            in_specs=[vmem] * (1 + len(got)),
            out_specs=[vmem] * nblk,
            compiler_params=params,
            name="tower_sum",
        )(keep, *got)
    else:
        by_part = keep.reshape(slots, ntow, items // ntow, width)
        total = lax.dynamic_index_in_dim(by_part, tow_me, 1, keepdims=False)
        for to, _, pattern in tow_peers:
            sent = lax.dynamic_index_in_dim(by_part, to, 1, keepdims=False)
            sent = sent.astype(jnp.bfloat16)
            total = total + lax.ppermute(sent, "tower", pattern).astype(jnp.float32)
        total = total.reshape(nblk, shard_rows, width)
        own = pick(total, blk_me)
        leaving = [pick(total, to).astype(jnp.bfloat16) for to, _, _ in blk_peers]
    own, *rest = (own, *leaving, *query_grads)
    leaving, query_grads = rest[: nblk - 1], rest[nblk - 1 :]
    if nblk == 4:
        (_, _, near), (_, _, over) = blk_peers[:2]
        to_near, to_over, to_far = leaving
        joined = pl.pallas_call(
            shard_sum_kernel,
            out_shape=pltpu.VMEM((shard_rows, width), jnp.bfloat16),
            in_specs=[vmem, vmem],
            out_specs=vmem,
            compiler_params=params,
            name="join",
        )(to_over, lax.ppermute(to_far, "blk", near))
        terms = [lax.ppermute(joined, "blk", over), lax.ppermute(to_near, "blk", near)]
    else:
        terms = [lax.ppermute(sent, "blk", p) for sent, (_, _, p) in zip(leaving, blk_peers)]
    panel_grads = pl.pallas_call(
        shard_sum_kernel,
        out_shape=jax.ShapeDtypeStruct((shard_rows, width), jnp.float32),
        in_specs=[vmem] * (1 + len(terms)),
        out_specs=vmem,
        compiler_params=params,
        cost_estimate=pl.CostEstimate(flops=10**9, bytes_accessed=10**7, transcendentals=0),
        name="shard_sum",
    )(own, *terms).reshape(shard, items // ntow, width)

    blocks = list(query_grads[:per])
    for n, (to, _, pattern) in enumerate(group_peers):
        home = [(d, s) for s, d in pattern]
        for block in query_grads[(n + 1) * per : (n + 2) * per]:
            blocks.append(lax.ppermute(block, "group", home))
    back_q, back_l = pl.pallas_call(
        functools.partial(home_kernel, per, functools.partial(partners, "group")),
        out_shape=[
            pltpu.HBM((nq, rows, width), jnp.bfloat16),
            jax.ShapeDtypeStruct((nq, rows), jnp.bfloat16),
        ],
        in_specs=[vmem] * nq,
        out_specs=[hbm, vmem],
        scratch_shapes=[pltpu.SemaphoreType.DMA((nq,))],
        compiler_params=params,
        name="home",
    )(*blocks)
    return back_l, back_q, panel_grads


def solution(mesh):
    return jax.shard_map(
        shards,
        mesh=mesh,
        in_specs=(
            P(("tower", "group", "blk"), None, None),
            P(("tower", "group", "blk"), None),
            P(("tower", "group", "blk"), None),
            P("group", None),
            P(("group", "blk"), None, None),
            P(("group", "blk"), None),
        ),
        out_specs=(
            P(("tower", "group", "blk"), None),
            P(("tower", "group", "blk"), None, None),
            P(("group", "blk"), "tower", None),
        ),
        check_vma=False,
    )
```

```python
import functools
import math

import jax
import jax.numpy as jnp
from jax import lax
from jax.experimental import pallas as pl
from jax.experimental.pallas import tpu as pltpu
from jax.sharding import PartitionSpec as P

VMEM_LIMIT = 40 * 1024 * 1024
LANES = 128
TILE = 16
ORDER = (
    (("g", 0), ("s", 0), ("p", 0)),
    (("g", 1), ("s", 1), ("e", 0), ("w", 0), ("t", 0), ("p", 1), ("q", 0), ("a", 0)),
    (),
)
LN2 = math.log(2.0)
COST = 10**10


def peers(axis):
    n = lax.axis_size(axis)
    me = lax.axis_index(axis)
    if n & (n - 1) == 0:
        return [(me ^ k, me ^ k, [(i, i ^ k) for i in range(n)]) for k in range(1, n)]
    return [
        (lax.rem(me + k, n), lax.rem(me + n - k, n), [(i, (i + k) % n) for i in range(n)])
        for k in range(1, n)
    ]


def pick(array, index):
    return lax.dynamic_index_in_dim(array, index, 0, keepdims=False)


def message_kernel(per, part_rows, targets, panels, scales, queries, ids_far, pos_far, *refs):
    (message, *outs, held, ids, positives, marks, sems) = refs
    rows, nsel = queries.shape[1], ids_far.shape[1]
    items, shard = scales.shape
    reps = rows // LANES
    copies = []

    def fetch(source, target):
        copies.append(pltpu.make_async_copy(source, target, sems.at[len(copies)]))
        copies[-1].start()

    start = pl.multiple_of(lax.axis_index("tower") * part_rows, TILE)
    fetch(ids_far, ids)
    fetch(pos_far, positives)
    fetch(scales, held)
    fetch(panels.at[pl.ds(start, part_rows), :], message.at[0:part_rows, :])
    goal = [to * per + i for to in targets() for i in range(per)]
    for block, out in zip(goal, outs):
        fetch(queries.at[block], out.at[0:rows, :])
    for copy in copies[:3]:
        copy.wait()
    below = pl.ds(part_rows, items)
    message[below, :] = jnp.zeros((items, message.shape[1]), message.dtype)
    message[below, 0:shard] = held[...]
    for block, out in zip(goal, outs):
        place = positives[pl.ds(block, 1), :]
        marks[...] = jnp.zeros_like(marks)
        for c in range(reps):
            chunk = place[:, c * LANES : (c + 1) * LANES]
            marks[c : c + 1, 0:LANES] = (chunk // items).astype(jnp.float32)
            marks[c : c + 1, LANES : 2 * LANES] = (chunk % items).astype(jnp.float32)
        marks[reps : reps + 1, 0:nsel] = ids[pl.ds(block, 1), :].astype(jnp.float32)
        out[rows : rows + TILE, :] = marks[...].astype(out.dtype)
    for copy in copies[3:]:
        copy.wait()


def list_kernel(items, count, *refs):
    messages, places, lists = refs[:count], refs[-2 * count : -count], refs[-count:]
    for message, place, ids in zip(messages, places, lists):
        rows = message.shape[0] - TILE
        reps = rows // LANES
        marks = message[rows : rows + TILE, :].astype(jnp.float32)
        found = [
            marks[n : n + 1, 0:LANES] * items + marks[n : n + 1, LANES : 2 * LANES]
            for n in range(reps)
        ]
        found = jnp.concatenate(found, axis=1).astype(jnp.int32)
        place[...] = jnp.broadcast_to(found, place.shape)
        ids[...] = jnp.broadcast_to(marks[reps : reps + 1, 0:LANES], ids.shape).astype(jnp.int32)


def score_kernel(dims, *refs):
    nq, nlocal, ntow, n_piece, rows, nsel, items, slots, shard, split = dims
    refs = list(refs)

    def take(n):
        out, refs[:] = refs[:n], refs[n:]
        return out

    owner_far, ids_far, pos_far, scale_far, queries, own = take(6)
    messages = take(nq - nlocal)
    places = take(nq - nlocal)
    lists = take(nq - nlocal)
    pieces = take(n_piece)
    outs = take(nq)
    (keep,) = take(1)
    sends = take(ntow - 1 if split else 0)
    (panel, wide, query, score, sel, sel_wide, weight, term, grad, place) = refs[:10]
    (owner, ids, far_ids, pos_own, scale_own, sems) = refs[10:]
    part = shard // ntow
    cand = nsel * items
    width = panel.shape[1]
    mine, blk_me, tow_me = lax.axis_index("group"), lax.axis_index("blk"), lax.axis_index("tower")
    blk_to = [to for _, to, _ in peers("blk")]
    tow_to = [to for _, to, _ in peers("tower")]
    copies = []

    def fetch(source, target):
        copies.append(pltpu.make_async_copy(source, target, sems.at[len(copies)]))
        copies[-1].start()
        return copies[-1]

    def rows_at(slot, count):
        return pl.ds(pl.multiple_of(slot * items, TILE), count * items)

    early = [fetch(ids_far, ids), fetch(owner_far, owner)]
    early.append(fetch(scale_far, scale_own))
    early.append(fetch(pos_far, pos_own))
    early.append(fetch(own, panel.at[rows_at(blk_me * shard, shard), :]))
    local = [fetch(queries.at[mine * nlocal + n], query.at[n]) for n in range(nlocal)]
    for n, piece in enumerate(pieces):
        first = blk_to[n // ntow] * shard + ([tow_me] + tow_to)[n % ntow] * part
        panel[rows_at(first, part), :] = piece[0 : part * items, :]
    grad[...] = jnp.zeros_like(grad)

    def block_rows(b):
        return query[b] if b < nlocal else messages[b - nlocal][0:rows, :]

    reps = rows // LANES
    moved = []

    for b in range(nlocal, nq):
        place[b] = places[b - nlocal][...]
        moved.append(fetch(lists[b - nlocal], far_ids.at[b]))
    early[2].wait()
    item_of = lax.broadcasted_iota(jnp.int32, (shard * items, items), 0) % items
    spread = item_of == lax.broadcasted_iota(jnp.int32, (shard * items, items), 1)
    spread = spread.astype(jnp.bfloat16)

    def widen(values, at):
        lanes = values.shape[1]
        of_item = jnp.dot(spread, values, preferred_element_type=jnp.float32)
        slot_of = lax.broadcasted_iota(jnp.int32, (shard * items, lanes), 0) // items
        mine = slot_of == lax.broadcasted_iota(jnp.int32, (shard * items, lanes), 1)
        wide[at, :] = jnp.dot(
            jnp.where(mine, of_item, 0.0).astype(jnp.bfloat16),
            jnp.ones((lanes, LANES), jnp.bfloat16),
            preferred_element_type=jnp.float32,
        ) * (1.0 / LN2)

    widen(scale_own[...], rows_at(blk_me * shard, shard))
    for n, to in enumerate(blk_to):
        widen(pieces[n * ntow][part * items : part * items + items, 0:LANES], rows_at(to * shard, shard))

    line = lax.broadcasted_iota(jnp.int32, (8, LANES), 0)
    state = [{} for _ in range(nq)]
    for n, copy in enumerate(early + local + moved):
        if n != 2:
            copy.wait()
    for b in range(nlocal):
        place[b] = jnp.broadcast_to(pos_own[pl.ds(mine * nlocal + b, 1), :], (8, rows))

    def slot_of(b, j):
        if b < nlocal:
            return owner[0, ids[mine * nlocal + b, j]]
        return owner[0, far_ids[b, 0, j]]

    def gather(b):
        two = b % 2
        for j in range(nsel):
            at = slice(j * items, (j + 1) * items)
            slot = rows_at(slot_of(b, j), 1)
            sel[two, at, :] = panel[slot, :]
            sel_wide[two, at, :] = wide[slot, :]

    def scores(b):
        score[b % 2] = lax.dot_general(
            sel[b % 2],
            block_rows(b),
            (((1,), (1,)), ((), ())),
            preferred_element_type=jnp.float32,
        )

    def spread_scale(two, first):
        return jnp.tile(sel_wide[two, first : first + 8, :], (1, reps))

    def is_positive(pos, first):
        return jnp.tile(line + first, (1, reps)) == pos

    def peaks(b):
        two = b % 2
        peak = jnp.full((8, rows), -jnp.inf, jnp.float32)
        for first in range(0, cand, 8):
            s = score[two, first : first + 8, :] * spread_scale(two, first)
            score[two, first : first + 8, :] = s
            peak = jnp.maximum(peak, s)
        state[b]["top"] = jnp.max(peak, axis=0, keepdims=True)

    def exps(b):
        two, top, pos = b % 2, state[b]["top"], place[b]
        total = jnp.zeros((8, rows), jnp.float32)
        pick = jnp.zeros((8, rows), jnp.float32)
        for first in range(0, cand, 8):
            s = score[two, first : first + 8, :]
            e = jnp.exp2(s - top)
            score[two, first : first + 8, :] = e
            total = total + e
            pick = jnp.where(is_positive(pos, first), s, pick)
        total = jnp.sum(total, axis=0, keepdims=True)
        picked = jnp.sum(pick, axis=0, keepdims=True)
        loss = (top - picked) * LN2 + jnp.log(total)
        state[b]["inverse"] = LN2 / total
        row_of = lax.broadcasted_iota(jnp.int32, (TILE, LANES), 0)
        below = jnp.zeros((TILE, LANES), jnp.float32)
        for n in range(reps):
            below = jnp.where(row_of == n, loss[:, n * LANES : (n + 1) * LANES], below)
        outs[b][rows : rows + TILE, :] = jnp.zeros((TILE, width), jnp.bfloat16)
        outs[b][rows : rows + TILE, 0:LANES] = below.astype(jnp.bfloat16)

    def weigh(b):
        two, inverse, pos = b % 2, state[b]["inverse"], place[b]
        for start in range(0, cand, TILE):
            halves = []
            for first in range(start, start + TILE, 8):
                chance = score[two, first : first + 8, :] * inverse
                chance = jnp.where(is_positive(pos, first), chance - LN2, chance)
                halves.append(chance * spread_scale(two, first))
            weight[two, start : start + TILE, :] = jnp.concatenate(halves, axis=0).astype(
                jnp.bfloat16
            )

    def panel_terms(b):
        term[b % 2] = jnp.dot(
            weight[b % 2], block_rows(b), preferred_element_type=jnp.float32
        )

    def scatter(b):
        for j in range(nsel):
            slot = slot_of(b, j)
            add = term[b % 2, j * items : (j + 1) * items, :]
            if split:
                grad[slot] += add.reshape(ntow, items // ntow, width)
            else:
                grad[rows_at(slot, 1), :] += add

    def query_terms(b):
        outs[b][0:rows, :] = lax.dot_general(
            weight[b % 2],
            sel[b % 2],
            (((0,), (0,)), ((), ())),
            preferred_element_type=jnp.float32,
        ).astype(jnp.bfloat16)

    jobs = dict(g=gather, s=scores, p=peaks, e=exps, w=weigh, t=panel_terms, a=scatter, q=query_terms)
    for name, shift in ORDER[0]:
        if shift < nq:
            jobs[name](shift)
    for b in range(nq):
        for name, shift in ORDER[1]:
            if 0 <= b + shift < nq:
                jobs[name](b + shift)
    for name, shift in ORDER[2]:
        jobs[name](nq - 1 + shift)
    if split:
        keep[...] = grad[:, tow_me].reshape(keep.shape)
        for to, send in zip([to for to, _, _ in peers("tower")], sends):
            send[...] = grad[:, to].reshape(send.shape).astype(send.dtype)
    else:
        keep[...] = grad[...]


def tower_sum_kernel(nblk, partners, keep, *refs):
    got, outs = refs[: len(refs) - nblk], refs[len(refs) - nblk :]
    me, to = partners()
    rows = keep.shape[0] // nblk
    for owner, out in zip([me] + to, outs):
        at = pl.ds(pl.multiple_of(owner * rows, TILE), rows)
        total = keep[at, :]
        for term in got:
            total = total + term[at, :].astype(jnp.float32)
        out[...] = total.astype(out.dtype)


def shard_sum_kernel(*refs):
    (*terms, out) = refs
    total = terms[0][...].astype(jnp.float32)
    for term in terms[1:]:
        total = total + term[...].astype(jnp.float32)
    out[...] = total.astype(out.dtype)


def land_kernel(block, out):
    out[...] = block[...]


def home_kernel(per, partners, *refs):
    (*blocks, grads, losses, sems) = refs
    nq, rows, _ = grads.shape
    me, to = partners()
    copies = []
    lines = lax.broadcasted_iota(jnp.int32, (nq, LANES), 0)
    parts = [jnp.zeros((nq, LANES), jnp.float32)] * (rows // LANES)
    for n, block in enumerate(blocks):
        place = ([me] + to)[n // per] * per + n % per
        copies.append(
            pltpu.make_async_copy(block.at[0:rows, :], grads.at[place], sems.at[n])
        )
        copies[-1].start()
    for n, block in enumerate(blocks):
        place = ([me] + to)[n // per] * per + n % per
        tile = block[rows : rows + TILE, 0:LANES].astype(jnp.float32)
        parts = [jnp.where(lines == place, tile[c : c + 1, :], p) for c, p in enumerate(parts)]
    losses[...] = jnp.concatenate(parts, axis=1).astype(losses.dtype)
    for copy in copies:
        copy.wait()


def shards(queries, cluster_ids, positives, owner_map, panels, scales):
    nq, rows, width = queries.shape
    shard, items = scales.shape
    nsel = cluster_ids.shape[1]
    nblk, ntow = lax.axis_size("blk"), lax.axis_size("tower")
    slots = shard * nblk
    part = shard // ntow
    cand = nsel * items
    ngroup = lax.axis_size("group")
    mine, blk_me, tow_me = lax.axis_index("group"), lax.axis_index("blk"), lax.axis_index("tower")
    group_peers, blk_peers, tow_peers = peers("group"), peers("blk"), peers("tower")
    per = nq // ngroup
    split = (items // ntow) % 8 == 0
    vmem = pl.BlockSpec(memory_space=pltpu.VMEM)
    hbm = pl.BlockSpec(memory_space=pltpu.HBM)
    pin = functools.partial(pltpu.with_memory_space_constraint, memory_space=pltpu.HBM)
    params = pltpu.CompilerParams(vmem_limit_bytes=VMEM_LIMIT)
    flat_panels = panels.reshape(shard * items, width)
    flat_scales = scales.T

    def targets():
        return [to for to, _, _ in peers("group")]

    message, *leaving = pl.pallas_call(
        functools.partial(message_kernel, per, part * items, targets),
        out_shape=[jax.ShapeDtypeStruct((part * items + items, width), panels.dtype)]
        + [jax.ShapeDtypeStruct((rows + TILE, width), queries.dtype)] * (nq - per),
        in_specs=[hbm] * 5,
        out_specs=[vmem] * (1 + nq - per),
        scratch_shapes=[
            pltpu.VMEM(flat_scales.shape, scales.dtype),
            pltpu.VMEM(cluster_ids.shape, jnp.int32),
            pltpu.VMEM(positives.shape, jnp.int32),
            pltpu.VMEM((TILE, width), jnp.float32),
            pltpu.SemaphoreType.DMA((4 + nq - per,)),
        ],
        compiler_params=params,
        name="messages",
    )(pin(flat_panels), pin(flat_scales), pin(queries), pin(cluster_ids), pin(positives))

    pieces = []
    near = [lax.ppermute(message, "blk", pattern) for _, _, pattern in blk_peers[:2]]
    for n, (_, _, pattern) in enumerate(blk_peers):
        if n < 2:
            piece = near[n]
        elif nblk == 4:
            piece = lax.ppermute(near[1], "blk", blk_peers[0][2])
        else:
            piece = lax.ppermute(message, "blk", pattern)
        pieces.append(piece)
        for _, tow_source, tow_pattern in tow_peers:
            pieces.append(lax.ppermute(piece, "tower", tow_pattern))

    arrived = [
        lax.ppermute(leaving[n * per + i], "group", pattern)
        for n, (_, _, pattern) in enumerate(group_peers)
        for i in range(per)
    ]
    far, first = nq - per, pieces[1:2]
    lists = pl.pallas_call(
        functools.partial(list_kernel, items, far),
        out_shape=[jax.ShapeDtypeStruct((8, rows), jnp.int32)] * far
        + [jax.ShapeDtypeStruct((8, LANES), jnp.int32)] * far,
        in_specs=[vmem] * (far + len(first)),
        out_specs=[vmem] * (2 * far),
        compiler_params=params,
        cost_estimate=pl.CostEstimate(flops=COST, bytes_accessed=COST // 1000, transcendentals=0),
        name="lists",
    )(*arrived, *first)
    dims = (nq, per, ntow, len(pieces), rows, nsel, items, slots, shard, split)
    sent_rows = slots * items // ntow
    keep_rows = sent_rows if split else slots * items
    n_send = ntow - 1 if split else 0
    grad_shape = (slots, ntow, items // ntow, width) if split else (slots * items, width)
    results = pl.pallas_call(
        functools.partial(score_kernel, dims),
        out_shape=[pltpu.VMEM((rows + TILE, width), jnp.bfloat16)] * nq
        + [pltpu.VMEM((keep_rows, width), jnp.float32)]
        + [pltpu.VMEM((sent_rows, width), jnp.bfloat16)] * n_send,
        in_specs=[hbm] * 6 + [vmem] * (3 * (nq - per) + len(pieces)),
        out_specs=[vmem] * (nq + 1 + n_send),
        scratch_shapes=[
            pltpu.VMEM((slots * items, width), jnp.bfloat16),
            pltpu.VMEM((slots * items, LANES), jnp.float32),
            pltpu.VMEM((per, rows, width), jnp.bfloat16),
            pltpu.VMEM((2, cand, rows), jnp.float32),
            pltpu.VMEM((2, cand, width), jnp.bfloat16),
            pltpu.VMEM((2, cand, LANES), jnp.float32),
            pltpu.VMEM((2, cand, rows), jnp.bfloat16),
            pltpu.VMEM((2, cand, width), jnp.float32),
            pltpu.VMEM(grad_shape, jnp.float32),
            pltpu.VMEM((nq, 8, rows), jnp.int32),
            pltpu.SMEM(owner_map.shape, jnp.int32),
            pltpu.SMEM(cluster_ids.shape, jnp.int32),
            pltpu.SMEM((nq, 8, LANES), jnp.int32),
            pltpu.VMEM(positives.shape, jnp.int32),
            pltpu.VMEM(flat_scales.shape, flat_scales.dtype),
            pltpu.SemaphoreType.DMA((5 + nq,)),
        ],
        compiler_params=params,
        name="score",
    )(
        pin(owner_map),
        pin(cluster_ids),
        pin(positives),
        pin(flat_scales),
        pin(queries),
        pin(flat_panels),
        *arrived,
        *lists,
        *pieces,
    )
    query_grads, keep, sends = results[:nq], results[nq], results[nq + 1 :]

    def partners(axis):
        return lax.axis_index(axis), [to for to, _, _ in peers(axis)]

    shard_rows = shard * items // ntow
    wide_terms = [nblk == 4 and n == 1 for n in range(nblk - 1)]
    if split:
        got = [lax.ppermute(sent, "tower", p) for sent, (_, _, p) in zip(sends, tow_peers)]
        own, *leaving = pl.pallas_call(
            functools.partial(tower_sum_kernel, nblk, functools.partial(partners, "blk")),
            out_shape=[pltpu.VMEM((shard_rows, width), jnp.float32)]
            + [
                pltpu.VMEM((shard_rows, width), jnp.float32 if stays else jnp.bfloat16)
                for stays in wide_terms
            ],
            in_specs=[vmem] * (1 + len(got)),
            out_specs=[vmem] * nblk,
            compiler_params=params,
            name="tower_sum",
        )(keep, *got)
    else:
        by_part = keep.reshape(slots, ntow, items // ntow, width)
        total = lax.dynamic_index_in_dim(by_part, tow_me, 1, keepdims=False)
        for to, _, pattern in tow_peers:
            sent = lax.dynamic_index_in_dim(by_part, to, 1, keepdims=False)
            sent = sent.astype(jnp.bfloat16)
            total = total + lax.ppermute(sent, "tower", pattern).astype(jnp.float32)
        total = total.reshape(nblk, shard_rows, width)
        own = pick(total, blk_me)
        leaving = [pick(total, to).astype(jnp.bfloat16) for to, _, _ in blk_peers]
    own, *rest = (own, *leaving, *query_grads)
    leaving, query_grads = rest[: nblk - 1], rest[nblk - 1 :]
    if nblk == 4:
        (_, _, near), (_, _, over) = blk_peers[:2]
        to_near, to_over, to_far = leaving
        joined = pl.pallas_call(
            shard_sum_kernel,
            out_shape=pltpu.VMEM((shard_rows, width), jnp.bfloat16),
            in_specs=[vmem, vmem],
            out_specs=vmem,
            compiler_params=params,
            name="join",
        )(to_over, lax.ppermute(to_far, "blk", near))
        terms = [lax.ppermute(joined, "blk", over), lax.ppermute(to_near, "blk", near)]
    else:
        terms = [lax.ppermute(sent, "blk", p) for sent, (_, _, p) in zip(leaving, blk_peers)]
    panel_grads = pl.pallas_call(
        shard_sum_kernel,
        out_shape=jax.ShapeDtypeStruct((shard_rows, width), jnp.float32),
        in_specs=[vmem] * (1 + len(terms)),
        out_specs=vmem,
        compiler_params=params,
        cost_estimate=pl.CostEstimate(flops=10**9, bytes_accessed=10**7, transcendentals=0),
        name="shard_sum",
    )(own, *terms).reshape(shard, items // ntow, width)

    blocks = list(query_grads[:per])
    for n, (to, _, pattern) in enumerate(group_peers):
        home = [(d, s) for s, d in pattern]
        for block in query_grads[(n + 1) * per : (n + 2) * per]:
            blocks.append(lax.ppermute(block, "group", home))
    blocks[-1] = pl.pallas_call(
        land_kernel,
        out_shape=jax.ShapeDtypeStruct(blocks[-1].shape, blocks[-1].dtype),
        in_specs=[vmem],
        out_specs=vmem,
        compiler_params=params,
        cost_estimate=pl.CostEstimate(flops=COST, bytes_accessed=COST // 1000, transcendentals=0),
        name="land",
    )(blocks[-1])
    back_q, back_l = pl.pallas_call(
        functools.partial(home_kernel, per, functools.partial(partners, "group")),
        out_shape=[
            pltpu.HBM((nq, rows, width), jnp.bfloat16),
            jax.ShapeDtypeStruct((nq, rows), jnp.bfloat16),
        ],
        in_specs=[vmem] * nq,
        out_specs=[hbm, vmem],
        scratch_shapes=[pltpu.SemaphoreType.DMA((nq,))],
        compiler_params=params,
        name="home",
    )(*blocks)
    return back_l, back_q, panel_grads


def solution(mesh):
    return jax.shard_map(
        shards,
        mesh=mesh,
        in_specs=(
            P(("tower", "group", "blk"), None, None),
            P(("tower", "group", "blk"), None),
            P(("tower", "group", "blk"), None),
            P("group", None),
            P(("group", "blk"), None, None),
            P(("group", "blk"), None),
        ),
        out_specs=(
            P(("tower", "group", "blk"), None),
            P(("tower", "group", "blk"), None, None),
            P(("group", "blk"), "tower", None),
        ),
        check_vma=False,
    )
```
